128 devices in a mesh: shot: 32 (over z, y, x_lo), xline: 4 (over x_hi, core).
Axes of the slice: x: 4 (x_hi: 2, x_lo: 2; x = x_hi * 2 + x_lo), y: 4, z: 4, core: 2. Of those that a mesh axis runs over, the one named last changes fastest.
Arguments:
- records: bfloat16 [4, 64, 256, 2048], P('xline', 'shot'), may hold values from -1.796875 to 1.796875
- targets: bfloat16 [2048, 128, 256], P('xline', 'shot'), may hold values from -1.796875 to 1.796875
- aperture: int32 [128, 4, 64], P('shot', 'xline'), may hold values from 0 to 255
Outputs:
- multiples: bfloat16 [2048, 128, 256], P('xline', 'shot')
The draws below stay inside these ranges and needn't reach their ends.
Inputs may be any that keep to these rules, and one draw needn't show every extreme that they name: An aperture entry is the receiver of the output shot at which the contributing source lies.
All inputs are finite; a program needn't handle non-finite values.
Results may differ from the reference program's by a relative error of at most 0.0071.
Values may be sent and summed in bfloat16 or wider, within the bound.
No kernel may reach another device: no remote copies, remote signals or barrier semaphores. Data moves between devices by JAX's collectives and lax.ppermute only.
A program may use at most 128 MiB of HBM per device.

```python
import math
import jax
import jax.numpy as jnp
from jax import lax

R = 256
NT = 2048
NF = 256
NS = 128
NC = 64
NL = 4


def with_ends(result, key, low, high):
    dims = result.shape
    index_at = [jax.random.randint(jax.random.fold_in(key, axis), (), 0, dims[axis]) for axis in range(len(dims))]
    result = result.at[tuple(index_at)].set(low)
    longest = dims.index(max(dims))
    index_at[longest] = (index_at[longest] + 1) % dims[longest]
    return result.at[tuple(index_at)].set(high)


def level_of(rng, extent, shards, least, high):
    level = 1.0
    for dim, parts in shards:
        steps = jax.random.uniform(jax.random.fold_in(jax.random.fold_in(rng, 6), dim), (parts,), jnp.float32, least / len(shards), high / len(shards))
        level = level * jnp.repeat(jnp.exp(steps), extent[dim] // parts).reshape((-1,) + (1,) * (len(extent) - 1 - dim))
    return level


def gaussian(own_key, dims, deviation, bound, cuts=(), held_as=jnp.bfloat16):
    result = deviation * jax.random.normal(own_key, dims, jnp.float32)
    if cuts:
        result = result * level_of(own_key, dims, cuts, -0.22, 0.18)
    return jnp.clip(result, -bound, bound).astype(held_as)


def setup_inputs(seed: int = 0) -> dict:
    splits = jax.random.split(jax.random.key(seed), 4)
    records = gaussian(splits[0], (NL, NC, R, NT), 0.3, 1.796875, ((0, 4), (1, 32)))
    targets = gaussian(splits[1], (NT, NS, R), 0.3, 1.796875, ((0, 4), (1, 32)))
    aperture = with_ends(jax.random.randint(splits[2], (NS, NL, NC), 0, R), jax.random.fold_in(splits[2], 1), 0, R - 1).astype(jnp.int32)
    return dict(records=records, targets=targets, aperture=aperture)


def forward_table():
    times_col = jnp.arange(NT, dtype=jnp.int32)[:, None]
    freq_row = jnp.arange(1, NF + 1, dtype=jnp.int32)[None, :]
    angles = (times_col * freq_row % NT).astype(jnp.float32) * (2.0 * math.pi / NT)
    normalizing_scale = 1.0 / math.sqrt(NT)
    return jnp.concatenate([jnp.cos(angles) * normalizing_scale, -jnp.sin(angles) * normalizing_scale], axis=1).astype(jnp.bfloat16)

def inverse_table():
    times_col = jnp.arange(NT, dtype=jnp.int32)[:, None]
    freq_row = jnp.arange(1, NF + 1, dtype=jnp.int32)[None, :]
    angles = (times_col * freq_row % NT).astype(jnp.float32) * (2.0 * math.pi / NT)
    normalizing_scale = 2.0 / math.sqrt(NT)
    stacked = jnp.stack([jnp.cos(angles) * normalizing_scale, -jnp.sin(angles) * normalizing_scale], axis=2)
    return stacked.reshape(NT, 2 * NF)

def complex_mixing(real_part, imag_part):
    upper = jnp.stack([real_part, -imag_part], axis=1)
    lower = jnp.stack([imag_part, real_part], axis=1)
    return jnp.stack([upper, lower], axis=0)

def reference(records, targets, aperture):
    forward_fourier = forward_table().astype(jnp.float32)
    desired_spectra = jnp.einsum('tsr,tp->srp', targets.astype(jnp.float32), forward_fourier).astype(jnp.bfloat16)
    running = jnp.zeros((NF, 2, NS, R), jnp.float32)
    receivers = jnp.arange(R, dtype=jnp.int32)
    for source_line in range(NL):
        trace_spectra = jnp.einsum('crt,tp->cpr', records[source_line].astype(jnp.float32), forward_fourier)
        trace_spectra = trace_spectra.astype(jnp.bfloat16).reshape(NC, 2, NF, R)
        onehot = (aperture[:, source_line, :, None] == receivers).astype(jnp.float32)
        picked = jnp.einsum('scr,srp->scp', onehot, desired_spectra.astype(jnp.float32))
        mixing = complex_mixing(picked[:, :, :NF], picked[:, :, NF:])
        running = running + jnp.einsum('qspcf,cpfr->fqsr', mixing, trace_spectra.astype(jnp.float32))
    flat_traces = running.reshape(2 * NF, NS * R)
    predicted = jnp.dot(inverse_table(), flat_traces, precision=lax.Precision.HIGHEST, preferred_element_type=jnp.float32)
    return predicted.reshape(NT, NS, R).astype(jnp.bfloat16)
```

```python
import jax
import jax.numpy as jnp
import ml_dtypes
import numpy as np
from jax import lax
from jax.sharding import Mesh, PartitionSpec as P

NT = 2048
NF = 256


def part_order():
    freq = np.arange(NF).reshape(2, 64, 1, 2)
    return np.concatenate([freq, freq + NF], axis=2).reshape(2 * NF)


def tables():
    angle = (np.arange(NT)[:, None] * np.arange(1, NF + 1)[None, :] % NT) * (2.0 * np.pi / NT)
    waves = np.concatenate([np.cos(angle), -np.sin(angle)], axis=1)[:, part_order()]
    forward = (waves / np.sqrt(NT)).astype(np.float32).astype(ml_dtypes.bfloat16)
    inverse = (waves * (2.0 / np.sqrt(NT))).astype(np.float32).astype(ml_dtypes.bfloat16)
    return forward, inverse


def on_device(records, targets, aperture):
    forward, inverse = tables()
    core = lax.axis_index("core")
    block = 2 * lax.axis_index("xh") + core
    swap = [(0, 1), (1, 0)]
    bf16 = jnp.bfloat16
    mine = aperture.reshape(4, 32, 2).transpose(0, 2, 1).reshape(4, 64).astype(bf16)
    index = lax.all_gather(mine, ("shot", "xh", "core"), axis=0, tiled=False)

    table_here = lax.dynamic_slice(
        jnp.asarray(forward), (512 * block, 0), (512, 512)
    )
    partial = jnp.einsum(
        "tp,tn->pn", table_here, targets.reshape(512, 1024), preferred_element_type=jnp.float32
    ).reshape(2, 256, 1024)
    keep = lax.dynamic_index_in_dim(partial, core, 0, keepdims=False)
    give = lax.dynamic_index_in_dim(partial, 1 - core, 0, keepdims=False)
    wanted = (keep + lax.ppermute(give, "core", swap)).astype(bf16)

    spectra = jnp.einsum(
        "tp,crt->pcr", jnp.asarray(forward), records[0], preferred_element_type=jnp.float32
    ).astype(bf16).reshape(2, 256, 512)
    keep = lax.dynamic_index_in_dim(spectra, core, 0, keepdims=False)
    give = lax.dynamic_index_in_dim(spectra, 1 - core, 0, keepdims=False)
    take = lax.ppermute(give, "core", swap)
    first = jnp.where(core == 0, keep, take)
    second = jnp.where(core == 0, take, keep)
    message = jnp.concatenate([first, second, wanted], axis=1).reshape(64, 4, 2048)
    got = lax.all_to_all(message, ("shot", "xh"), 0, 0, tiled=True)

    gathers = got[:, :, :1024].reshape(32, 2, 4, 2, 2, 256)
    gathers = gathers.transpose(2, 1, 3, 4, 0, 5).reshape(4, 256, 256)
    shots = got[:, :, 1024:].reshape(32, 2, 4, 4, 256).astype(jnp.float32).sum(1)
    shots = shots.transpose(1, 0, 2, 3).reshape(4, 128, 256)
    index = index.reshape(32, 4, 4, 64).transpose(0, 2, 1, 3).reshape(128, 256).astype(jnp.int32)
    picked = jnp.take_along_axis(shots, index[None], axis=2).astype(bf16)
    pr, pi = picked[:2], picked[2:]
    left = jnp.concatenate(
        [jnp.concatenate([pr, -pi], axis=2), jnp.concatenate([pi, pr], axis=2)], axis=1
    )
    right = jnp.concatenate([gathers[:2], gathers[2:]], axis=1)
    running = jnp.einsum("fmk,fkr->fmr", left, right, preferred_element_type=jnp.float32).astype(bf16)
    running = running.reshape(2, 2, 32, 4, 256).transpose(2, 1, 0, 3, 4).reshape(32, 1, 4, 1024)
    running = jnp.broadcast_to(running, (32, 2, 4, 1024)).reshape(64, 4, 1024)
    back = lax.all_to_all(running, ("shot", "xh"), 0, 0, tiled=True).reshape(256, 1024)
    other = lax.ppermute(back, "core", swap)
    low = jnp.where(core == 0, back, other)
    high = jnp.where(core == 0, other, back)
    waves = lax.dynamic_slice(jnp.asarray(inverse), (512 * block, 0), (512, 512))
    out = jnp.dot(waves, jnp.concatenate([low, high], axis=0), preferred_element_type=jnp.float32)
    return out.astype(bf16).reshape(512, 4, 256)


def solution(mesh):
    devices = mesh.devices.reshape(32, 2, 2)
    cut = Mesh(devices, ("shot", "xh", "core"))
    xline = ("xh", "core")
    return jax.shard_map(
        on_device,
        mesh=cut,
        in_specs=(P(xline, "shot", None, None), P(xline, "shot", None), P("shot", xline, None)),
        out_specs=P(xline, "shot", None),
        check_vma=False,
    )
```

```python
import jax
import jax.numpy as jnp
import ml_dtypes
import numpy as np
from jax import lax
from jax.experimental import pallas as pl
from jax.experimental.pallas import tpu as pltpu
from jax.sharding import Mesh, PartitionSpec as P

NT = 2048
NF = 256
BF16 = jnp.bfloat16
F32 = jnp.float32
VMEM = pl.BlockSpec(memory_space=pltpu.VMEM)
ANY = pl.BlockSpec(memory_space=pl.ANY)
PARAMS = pltpu.CompilerParams(vmem_limit_bytes=48 * 2**20)


def part_order():
    freq = np.arange(NF).reshape(2, 64, 1, 2)
    return np.concatenate([freq, freq + NF], axis=2).reshape(2 * NF)


def tables():
    angle = (np.arange(NT)[:, None] * np.arange(1, NF + 1)[None, :] % NT) * (2.0 * np.pi / NT)
    waves = np.concatenate([np.cos(angle), -np.sin(angle)], axis=1)[:, part_order()]
    forward = (waves / np.sqrt(NT)).astype(np.float32).astype(ml_dtypes.bfloat16)
    inverse = (waves * (2.0 / np.sqrt(NT))).astype(np.float32).astype(ml_dtypes.bfloat16)
    return np.ascontiguousarray(forward.T), inverse


def one_hot(rows, depth):
    return np.eye(depth, dtype=np.float32)[np.asarray(rows).reshape(-1)].astype(ml_dtypes.bfloat16)


SHOT_MAJOR = one_hot(np.arange(256).reshape(64, 4).T, 256)
TIME_MAJOR = one_hot(np.arange(256).reshape(4, 64).T, 256)
PART_MAJOR = one_hot(np.arange(256).reshape(32, 2, 4).transpose(2, 1, 0), 256)
SPREAD = one_hot(np.broadcast_to(np.arange(128).reshape(4, 32).T[:, None, :], (32, 2, 4)), 128)
GATHER_MAJOR = np.ascontiguousarray(one_hot(np.arange(64).reshape(32, 2).T, 64).T)


def across(a, b):
    return lax.dot_general(a, b, (((1,), (1,)), ((), ())), preferred_element_type=F32)


def records_kernel(records_ref, table_ref, aperture_ref, gather_ref, give_ref, keep_ref, picks_ref, rec, tab, sems):
    core = lax.axis_index("core")
    copies = []
    for i, half in enumerate((1 - core, core)):
        copies.append(
            pltpu.make_async_copy(
                table_ref.at[pl.ds(pl.multiple_of(half * 256, 256), 256)], tab.at[i], sems.at[i]
            )
        )
    for c in range(2):
        copies.append(pltpu.make_async_copy(records_ref.at[0, c], rec.at[c], sems.at[2 + c]))
    for i in (0, 2, 3, 1):
        copies[i].start()
    picks = jnp.dot(
        aperture_ref[...].reshape(4, 64).astype(F32).astype(BF16), gather_ref[...], preferred_element_type=F32
    ).astype(BF16)
    picks_ref[...] = picks
    give_ref[256:272, :] = jnp.zeros((16, 512), BF16)
    give_ref[256:260, 0:64] = picks
    copies[0].wait()
    for c in range(2):
        copies[2 + c].wait()
        give_ref[0:256, 256 * c : 256 * c + 256] = across(tab[0], rec[c]).astype(BF16)
    copies[1].wait()
    for c in range(2):
        keep_ref[:, 256 * c : 256 * c + 256] = across(tab[1], rec[c]).astype(BF16)


def transform_records(records, table, aperture):
    return pl.pallas_call(
        records_kernel,
        out_shape=(
            jax.ShapeDtypeStruct((272, 512), BF16),
            jax.ShapeDtypeStruct((256, 512), BF16),
            jax.ShapeDtypeStruct((4, 64), BF16),
        ),
        in_specs=[ANY, ANY, VMEM, VMEM],
        out_specs=(VMEM, VMEM, VMEM),
        scratch_shapes=[
            pltpu.VMEM((2, 256, NT), BF16),
            pltpu.VMEM((2, 256, NT), BF16),
            pltpu.SemaphoreType.DMA((4,)),
        ],
        compiler_params=PARAMS,
        cost_estimate=pl.CostEstimate(flops=2**30, bytes_accessed=5 * 2**20, transcendentals=0),
        name="records",
    )(records, table, aperture, GATHER_MAJOR)


def targets_kernel(own_ref, other_ref, table_ref, keep_ref, order_ref, out_ref, raw, flat, tab, sems):
    core = lax.axis_index("core")
    block = 2 * lax.axis_index("xh") + core
    sibling = 2 * lax.axis_index("xh") + 1 - core
    copies = []
    for i, (part, at) in enumerate(((own_ref, block), (other_ref, sibling))):
        copies.append(pltpu.make_async_copy(part, raw.at[i], sems.at[2 * i]))
        copies.append(
            pltpu.make_async_copy(
                table_ref.at[
                    pl.ds(pl.multiple_of(core * 256, 256), 256), pl.ds(pl.multiple_of(at * 512, 512), 512)
                ],
                tab.at[i],
                sems.at[2 * i + 1],
            )
        )
    for copy in copies:
        copy.start()
    out_ref[:, :, 0:512] = keep_ref[...].reshape(64, 4, 512)
    total = None
    for i in range(2):
        copies[2 * i].wait()
        for t in range(8):
            rows = jnp.dot(
                order_ref[...], raw[i, 64 * t : 64 * t + 64].reshape(256, 256), preferred_element_type=F32
            ).astype(BF16)
            for s in range(4):
                flat[512 * i + 64 * t : 512 * i + 64 * t + 64, 256 * s : 256 * s + 256] = rows[64 * s : 64 * s + 64]
        copies[2 * i + 1].wait()
        part = jnp.dot(tab[i], flat[512 * i : 512 * i + 512], preferred_element_type=F32)
        total = part if total is None else total + part
    out_ref[:, :, 1024:2048] = total.astype(BF16).reshape(64, 4, 1024)


def transform_targets(own, other, table, keep):
    return pl.pallas_call(
        targets_kernel,
        out_shape=jax.ShapeDtypeStruct((64, 4, 2176), BF16),
        in_specs=[ANY, ANY, ANY, VMEM, VMEM],
        out_specs=VMEM,
        scratch_shapes=[
            pltpu.VMEM((2, 512, 4, 256), BF16),
            pltpu.VMEM((1024, 1024), BF16),
            pltpu.VMEM((2, 256, 512), BF16),
            pltpu.SemaphoreType.DMA((4,)),
        ],
        compiler_params=PARAMS,
        cost_estimate=pl.CostEstimate(flops=2**30, bytes_accessed=4 * 2**20, transcendentals=0),
        name="targets",
    )(own, other, table, keep, SHOT_MAJOR)


def fill_kernel(message_ref, taken_ref, picks_ref, out_ref, block, picks, sems):
    block[...] = taken_ref[0:256, :].reshape(64, 4, 512)
    both = jnp.concatenate([picks_ref[...], taken_ref[256:260, 0:64]], axis=1)
    picks[...] = jnp.broadcast_to(both[None], (64, 4, 128))
    first = pltpu.make_async_copy(block, out_ref.at[:, :, 512:1024], sems.at[0])
    second = pltpu.make_async_copy(picks, out_ref.at[:, :, 2048:2176], sems.at[1])
    first.start()
    second.start()
    first.wait()
    second.wait()


def fill(message, taken, picks):
    return pl.pallas_call(
        fill_kernel,
        out_shape=jax.ShapeDtypeStruct((64, 4, 2176), BF16),
        in_specs=[ANY, VMEM, VMEM],
        out_specs=ANY,
        scratch_shapes=[
            pltpu.VMEM((64, 4, 512), BF16),
            pltpu.VMEM((64, 4, 128), BF16),
            pltpu.SemaphoreType.DMA((2,)),
        ],
        input_output_aliases={0: 0},
        compiler_params=PARAMS,
        name="fill",
    )(message, taken, picks)


def lane_pick(low, high, index):
    inside = index & 127
    a = jnp.take_along_axis(low, inside, axis=1, mode="promise_in_bounds")
    b = jnp.take_along_axis(high, inside, axis=1, mode="promise_in_bounds")
    return jnp.where(index < 128, a, b)


def mix_kernel(got_ref, order_ref, spread_ref, out_ref, rows_ref):
    rows_ref[...] = jnp.dot(order_ref[...], got_ref[...].reshape(256, 2176), preferred_element_type=F32)
    index = [
        [rows_ref[64 * s + 32 * h : 64 * s + 32 * h + 32, 2048:2176].astype(jnp.int32) for h in range(2)]
        for s in range(4)
    ]
    picks, gathers = [], []
    for p in range(4):
        parts = []
        for s in range(4):
            at = 1024 + 256 * s
            both = rows_ref[64 * p : 64 * p + 32, at : at + 256] + rows_ref[64 * p + 32 : 64 * p + 64, at : at + 256]
            parts.append(
                jnp.concatenate([lane_pick(both[:, :128], both[:, 128:], index[s][h]) for h in range(2)], axis=1)
            )
        picks.append(jnp.concatenate(parts, axis=0))
        gathers.append(
            jnp.concatenate(
                [
                    rows_ref[64 * p + 32 * h : 64 * p + 32 * h + 32, 256 * b : 256 * b + 256].astype(BF16)
                    for h in range(2)
                    for b in range(4)
                ],
                axis=0,
            )
        )
    total = [None] * 4
    for f in range(2):
        re, im, minus = picks[f].astype(BF16), picks[2 + f].astype(BF16), (-picks[2 + f]).astype(BF16)
        left = jnp.concatenate(
            [jnp.concatenate([re, minus], axis=1), jnp.concatenate([im, re], axis=1)], axis=0
        )
        right = jnp.concatenate([gathers[f], gathers[2 + f]], axis=0)
        out = jnp.dot(left, right, preferred_element_type=F32).astype(BF16)
        for part in range(2):
            total[2 * part + f] = jnp.concatenate(
                [out[128 * part + 32 * s : 128 * part + 32 * s + 32] for s in range(4)], axis=1
            )
    total = jnp.concatenate(total, axis=0)
    out_ref[...] = (
        jnp.dot(spread_ref[...], total, preferred_element_type=F32).astype(BF16).reshape(64, 4, 1024)
    )


def mix(got):
    return pl.pallas_call(
        mix_kernel,
        out_shape=jax.ShapeDtypeStruct((64, 4, 1024), BF16),
        in_specs=[VMEM, VMEM, VMEM],
        out_specs=VMEM,
        scratch_shapes=[pltpu.VMEM((256, 2176), F32)],
        compiler_params=PARAMS,
        name="mix",
    )(got, PART_MAJOR, SPREAD)


def inverse_kernel(own_ref, other_ref, table_ref, order_ref, out_ref, tab, sem):
    core = lax.axis_index("core")
    block = 2 * lax.axis_index("xh") + core
    copy = pltpu.make_async_copy(table_ref.at[pl.ds(pl.multiple_of(block * 512, 512), 512)], tab, sem)
    copy.start()
    own = own_ref[...].reshape(256, 1024)
    other = other_ref[...].reshape(256, 1024)
    copy.wait()
    for half in range(2):
        rows = pl.ds(256 * half, 256)
        here = jnp.dot(tab[rows, pl.ds(pl.multiple_of(core * 256, 256), 256)], own, preferred_element_type=F32)
        here += jnp.dot(
            tab[rows, pl.ds(pl.multiple_of((1 - core) * 256, 256), 256)], other, preferred_element_type=F32
        )
        here = here.astype(BF16)
        for t in range(4):
            stack = jnp.concatenate(
                [here[64 * t : 64 * t + 64, 256 * s : 256 * s + 256] for s in range(4)], axis=0
            )
            out_ref[256 * half + 64 * t : 256 * half + 64 * t + 64] = (
                jnp.dot(order_ref[...], stack, preferred_element_type=F32).astype(BF16).reshape(64, 4, 256)
            )


def transform_back(own, other, table):
    return pl.pallas_call(
        inverse_kernel,
        out_shape=jax.ShapeDtypeStruct((512, 4, 256), BF16),
        in_specs=[VMEM, VMEM, ANY, VMEM],
        out_specs=VMEM,
        scratch_shapes=[pltpu.VMEM((512, 512), BF16), pltpu.SemaphoreType.DMA],
        compiler_params=PARAMS,
        name="inverse",
    )(own, other, table, TIME_MAJOR)


def on_device(records, targets, aperture):
    forward, inverse = tables()
    swap = [(0, 1), (1, 0)]
    others = lax.ppermute(targets, "core", swap)
    give, keep, picks = transform_records(records, forward, aperture)
    taken = lax.ppermute(give, "core", swap)
    message = transform_targets(targets, others, forward, keep)
    message = fill(message, taken, picks)
    got = lax.all_to_all(message, ("shot", "xh"), 0, 0, tiled=True)
    back = lax.all_to_all(mix(got), ("shot", "xh"), 0, 0, tiled=True)
    return transform_back(back, lax.ppermute(back, "core", swap), inverse)


def solution(mesh):
    cut = Mesh(mesh.devices.reshape(32, 2, 2), ("shot", "xh", "core"))
    xline = ("xh", "core")
    return jax.shard_map(
        on_device,
        mesh=cut,
        in_specs=(P(xline, "shot", None, None), P(xline, "shot", None), P("shot", xline, None)),
        out_specs=P(xline, "shot", None),
        check_vma=False,
    )
```

```python
import jax
import jax.numpy as jnp
import ml_dtypes
import numpy as np
from jax import lax
from jax.experimental import pallas as pl
from jax.experimental.pallas import tpu as pltpu
from jax.sharding import Mesh, PartitionSpec as P

NT = 2048
NF = 256
BF16 = jnp.bfloat16
F32 = jnp.float32
VMEM = pl.BlockSpec(memory_space=pltpu.VMEM)
ANY = pl.BlockSpec(memory_space=pl.ANY)
PARAMS = pltpu.CompilerParams(vmem_limit_bytes=48 * 2**20)


def part_order():
    freq = np.arange(NF).reshape(2, 64, 1, 2)
    return np.concatenate([freq, freq + NF], axis=2).reshape(2 * NF)


def tables():
    angle = (np.arange(NT)[:, None] * np.arange(1, NF + 1)[None, :] % NT) * (2.0 * np.pi / NT)
    waves = np.concatenate([np.cos(angle), -np.sin(angle)], axis=1)[:, part_order()]
    forward = (waves / np.sqrt(NT)).astype(np.float32).astype(ml_dtypes.bfloat16)
    inverse = (waves * (2.0 / np.sqrt(NT))).astype(np.float32).astype(ml_dtypes.bfloat16)
    first = forward[: NT // 2]
    return np.ascontiguousarray(first.reshape(NT // 2, 2, 256).transpose(1, 0, 2)), np.ascontiguousarray(first.T), inverse


def one_hot(rows, depth):
    return np.eye(depth, dtype=np.float32)[np.asarray(rows).reshape(-1)].astype(ml_dtypes.bfloat16)


SHOT_MAJOR = one_hot(np.arange(256).reshape(64, 4).T, 256)
TIME_MAJOR = one_hot(np.arange(256).reshape(4, 64).T, 256)
PART_MAJOR = one_hot(np.arange(256).reshape(32, 2, 4).transpose(2, 1, 0), 256)
SPREAD = one_hot(np.broadcast_to(np.arange(128).reshape(4, 32).T[:, None, :], (32, 2, 4)), 128)
WIDE = NT // 4


def held(x):
    return pltpu.with_memory_space_constraint(x, pltpu.HBM)


def records_kernel(
    records_ref, table_ref, flipped_ref, aperture_ref, give_ref, keep_ref, picks_ref, piece_ref, rec, tab, ape, sems
):
    core = lax.axis_index("core")
    halves = (1 - core, core)
    lanes = [pl.ds(k * WIDE, WIDE) for k in (0, 2, 1, 3)]
    waits = []
    for k in range(4):
        waits.append([pltpu.make_async_copy(records_ref.at[0, :, :, lanes[k]], rec.at[k], sems.at[k, 2])])
        if k % 2 == 0:
            waits[k] += [
                pltpu.make_async_copy(table_ref.at[half, lanes[k]], tab.at[k // 2, i], sems.at[k, i])
                for i, half in enumerate(halves)
            ]
        for copy in waits[k]:
            copy.start()
    small = pltpu.make_async_copy(aperture_ref, ape, sems.at[4, 0])
    small.start()
    later = pltpu.make_async_copy(
        flipped_ref.at[pl.ds(pl.multiple_of(core * 256, 256), 256)], piece_ref, sems.at[4, 1]
    )
    later.start()
    c = lax.broadcasted_iota(jnp.int32, (64, 64), 0)
    j = lax.broadcasted_iota(jnp.int32, (64, 64), 1)
    order = (c == 2 * (j & 31) + (j >> 5)).astype(F32).astype(BF16)
    sign = (2 * (lax.broadcasted_iota(jnp.int32, (1, 256), 1) & 1) - 1).astype(F32).astype(BF16)
    total = [None, None]
    for k in range(4):
        for copy in waits[k]:
            copy.wait()
        for i in range(2):
            waves = tab[k // 2, i]
            if k % 2 == 1:
                waves = waves * sign
            part = jnp.dot(rec[k].reshape(512, WIDE), waves, preferred_element_type=F32)
            total[i] = part if total[i] is None else total[i] + part
    small.wait()
    picks = jnp.dot(ape[...].reshape(4, 64).astype(F32).astype(BF16), order, preferred_element_type=F32).astype(BF16)
    picks_ref[...] = picks
    give_ref[0:256, :] = total[0].T.astype(BF16)
    give_ref[256:272, :] = jnp.zeros((16, 512), BF16)
    give_ref[256:260, 0:64] = picks
    keep_ref[...] = total[1].T.astype(BF16)
    later.wait()


def transform_records(records, table, flipped, aperture):
    return pl.pallas_call(
        records_kernel,
        out_shape=(
            jax.ShapeDtypeStruct((272, 512), BF16),
            jax.ShapeDtypeStruct((256, 512), BF16),
            jax.ShapeDtypeStruct((4, 64), BF16),
            jax.ShapeDtypeStruct((256, 1024), BF16),
        ),
        in_specs=[ANY, ANY, ANY, ANY],
        out_specs=(VMEM, VMEM, VMEM, VMEM),
        scratch_shapes=[
            pltpu.VMEM((4, 2, 256, WIDE), BF16),
            pltpu.VMEM((2, 2, WIDE, 256), BF16),
            pltpu.VMEM((4, 1, 64), jnp.int32),
            pltpu.SemaphoreType.DMA((5, 3)),
        ],
        compiler_params=PARAMS,
        cost_estimate=pl.CostEstimate(flops=2**30, bytes_accessed=5 * 2**20, transcendentals=0),
        name="records",
    )(held(records), held(table), held(flipped), held(aperture))


def targets_kernel(own_ref, other_ref, piece_ref, keep_ref, order_ref, out_ref, flat):
    core = lax.axis_index("core")
    out_ref[:, :, 0:512] = keep_ref[...].reshape(64, 4, 512)
    total = None
    for i, raw_ref in enumerate((own_ref, other_ref)):
        for t in range(8):
            rows = jnp.dot(
                order_ref[...], raw_ref[64 * t : 64 * t + 64].reshape(256, 256), preferred_element_type=F32
            ).astype(BF16)
            for s in range(4):
                flat[i, 64 * t : 64 * t + 64, 256 * s : 256 * s + 256] = rows[64 * s : 64 * s + 64]
        at = core if i == 0 else 1 - core
        waves = piece_ref[:, pl.ds(pl.multiple_of(at * 512, 512), 512)]
        part = jnp.dot(waves, flat[i], preferred_element_type=F32)
        total = part if total is None else total + part
    odd = 1 - (lax.broadcasted_iota(jnp.int32, (256, 1), 0) & 1)
    total = total * (1 - 2 * odd * lax.axis_index("xh")).astype(F32)
    out_ref[:, :, 1024:2048] = total.astype(BF16).reshape(64, 4, 1024)


def transform_targets(own, other, piece, keep):
    return pl.pallas_call(
        targets_kernel,
        out_shape=jax.ShapeDtypeStruct((64, 4, 2176), BF16),
        in_specs=[VMEM, VMEM, VMEM, VMEM, VMEM],
        out_specs=VMEM,
        scratch_shapes=[pltpu.VMEM((2, 512, 1024), BF16)],
        compiler_params=PARAMS,
        cost_estimate=pl.CostEstimate(flops=2**30, bytes_accessed=4 * 2**20, transcendentals=0),
        name="targets",
    )(own, other, piece, keep, SHOT_MAJOR)


def fill_kernel(message_ref, taken_ref, picks_ref, out_ref, block, picks, sems):
    block[...] = taken_ref[0:256, :].reshape(64, 4, 512)
    both = jnp.concatenate([picks_ref[...], taken_ref[256:260, 0:64]], axis=1)
    picks[...] = jnp.broadcast_to(both[None], (64, 4, 128))
    first = pltpu.make_async_copy(block, out_ref.at[:, :, 512:1024], sems.at[0])
    second = pltpu.make_async_copy(picks, out_ref.at[:, :, 2048:2176], sems.at[1])
    first.start()
    second.start()
    first.wait()
    second.wait()


def fill(message, taken, picks):
    return pl.pallas_call(
        fill_kernel,
        out_shape=jax.ShapeDtypeStruct((64, 4, 2176), BF16),
        in_specs=[ANY, VMEM, VMEM],
        out_specs=ANY,
        scratch_shapes=[
            pltpu.VMEM((64, 4, 512), BF16),
            pltpu.VMEM((64, 4, 128), BF16),
            pltpu.SemaphoreType.DMA((2,)),
        ],
        input_output_aliases={0: 0},
        compiler_params=PARAMS,
        name="fill",
    )(message, taken, picks)


def lane_pick(low, high, index):
    inside = index & 127
    a = jnp.take_along_axis(low, inside, axis=1, mode="promise_in_bounds")
    b = jnp.take_along_axis(high, inside, axis=1, mode="promise_in_bounds")
    return jnp.where(index < 128, a, b)


def mix_kernel(got_ref, order_ref, spread_ref, out_ref, rows_ref):
    rows_ref[...] = jnp.dot(order_ref[...], got_ref[...].reshape(256, 2176), preferred_element_type=F32)
    index = [
        [rows_ref[64 * s + 32 * h : 64 * s + 32 * h + 32, 2048:2176].astype(jnp.int32) for h in range(2)]
        for s in range(4)
    ]
    picks, gathers = [], []
    for p in range(4):
        parts = []
        for s in range(4):
            at = 1024 + 256 * s
            both = rows_ref[64 * p : 64 * p + 32, at : at + 256] + rows_ref[64 * p + 32 : 64 * p + 64, at : at + 256]
            parts.append(
                jnp.concatenate([lane_pick(both[:, :128], both[:, 128:], index[s][h]) for h in range(2)], axis=1)
            )
        picks.append(jnp.concatenate(parts, axis=0))
        gathers.append(
            jnp.concatenate(
                [
                    rows_ref[64 * p + 32 * h : 64 * p + 32 * h + 32, 256 * b : 256 * b + 256].astype(BF16)
                    for h in range(2)
                    for b in range(4)
                ],
                axis=0,
            )
        )
    total = [None] * 4
    for f in range(2):
        re, im, minus = picks[f].astype(BF16), picks[2 + f].astype(BF16), (-picks[2 + f]).astype(BF16)
        left = jnp.concatenate(
            [jnp.concatenate([re, minus], axis=1), jnp.concatenate([im, re], axis=1)], axis=0
        )
        right = jnp.concatenate([gathers[f], gathers[2 + f]], axis=0)
        out = jnp.dot(left, right, preferred_element_type=F32).astype(BF16)
        for part in range(2):
            total[2 * part + f] = jnp.concatenate(
                [out[128 * part + 32 * s : 128 * part + 32 * s + 32] for s in range(4)], axis=1
            )
    total = jnp.concatenate(total, axis=0)
    out_ref[...] = (
        jnp.dot(spread_ref[...], total, preferred_element_type=F32).astype(BF16).reshape(64, 4, 1024)
    )


def mix(got):
    return pl.pallas_call(
        mix_kernel,
        out_shape=jax.ShapeDtypeStruct((64, 4, 1024), BF16),
        in_specs=[VMEM, VMEM, VMEM],
        out_specs=VMEM,
        scratch_shapes=[pltpu.VMEM((256, 2176), F32)],
        compiler_params=PARAMS,
        name="mix",
    )(got, PART_MAJOR, SPREAD)


def inverse_waves(table_ref, half, rows, count):
    block = 2 * lax.axis_index("xh") + lax.axis_index("core")
    return table_ref[
        pl.ds(pl.multiple_of(block * 512 + rows, 256), count), pl.ds(pl.multiple_of(half * 256, 256), 256)
    ]


def own_half_kernel(own_ref, table_ref, out_ref):
    waves = inverse_waves(table_ref, lax.axis_index("core"), 0, 512)
    out_ref[...] = jnp.dot(waves, own_ref[...].reshape(256, 1024), preferred_element_type=F32)


def own_half(own, table):
    return pl.pallas_call(
        own_half_kernel,
        out_shape=jax.ShapeDtypeStruct((512, 1024), F32),
        in_specs=[VMEM, VMEM],
        out_specs=VMEM,
        compiler_params=PARAMS,
        cost_estimate=pl.CostEstimate(flops=2**28, bytes_accessed=2**20, transcendentals=0),
        name="own_half",
    )(own, table)


def inverse_kernel(part_ref, other_ref, table_ref, order_ref, out_ref, ready, sems):
    other = other_ref[...].reshape(256, 1024)
    outs = []
    for half in range(2):
        waves = inverse_waves(table_ref, 1 - lax.axis_index("core"), 256 * half, 256)
        here = jnp.dot(waves, other, preferred_element_type=F32)
        here = (here + part_ref[256 * half : 256 * half + 256]).astype(BF16)
        for t in range(4):
            at = 256 * half + 64 * t
            stack = jnp.concatenate(
                [here[64 * t : 64 * t + 64, 256 * s : 256 * s + 256] for s in range(4)], axis=0
            )
            ready[at : at + 64] = (
                jnp.dot(order_ref[...], stack, preferred_element_type=F32).astype(BF16).reshape(64, 4, 256)
            )
            if t % 2 == 1:
                rows = pl.ds(at - 64, 128)
                outs.append(pltpu.make_async_copy(ready.at[rows], out_ref.at[rows], sems.at[len(outs)]))
                outs[-1].start()
    for copy in outs:
        copy.wait()


def transform_back(part, other, table):
    return pl.pallas_call(
        inverse_kernel,
        out_shape=jax.ShapeDtypeStruct((512, 4, 256), BF16),
        in_specs=[VMEM, VMEM, VMEM, VMEM],
        out_specs=ANY,
        scratch_shapes=[pltpu.VMEM((512, 4, 256), BF16), pltpu.SemaphoreType.DMA((4,))],
        compiler_params=PARAMS,
        name="inverse",
    )(part, other, table, TIME_MAJOR)


def on_device(records, targets, aperture):
    forward, flipped, inverse = tables()
    swap = [(0, 1), (1, 0)]
    others = lax.ppermute(targets, "core", swap)
    give, keep, picks, piece = transform_records(records, forward, flipped, aperture)
    taken = lax.ppermute(give, "core", swap)
    message = transform_targets(targets, others, piece, keep)
    message = fill(message, taken, picks)
    got = lax.all_to_all(message, ("shot", "xh"), 0, 0, tiled=True)
    back = lax.all_to_all(mix(got), ("shot", "xh"), 0, 0, tiled=True)
    other = lax.ppermute(back, "core", swap)
    return transform_back(own_half(back, inverse), other, inverse)


def solution(mesh):
    cut = Mesh(mesh.devices.reshape(32, 2, 2), ("shot", "xh", "core"))
    xline = ("xh", "core")
    return jax.shard_map(
        on_device,
        mesh=cut,
        in_specs=(P(xline, "shot", None, None), P(xline, "shot", None), P("shot", xline, None)),
        out_specs=P(xline, "shot", None),
        check_vma=False,
    )
```

```python
import jax
import jax.numpy as jnp
import ml_dtypes
import numpy as np
from jax import lax
from jax.experimental import pallas as pl
from jax.experimental.pallas import tpu as pltpu
from jax.sharding import Mesh, PartitionSpec as P

NT = 2048
NF = 256
BF16 = jnp.bfloat16
F32 = jnp.float32
VMEM = pl.BlockSpec(memory_space=pltpu.VMEM)
ANY = pl.BlockSpec(memory_space=pl.ANY)
PARAMS = pltpu.CompilerParams(vmem_limit_bytes=48 * 2**20)


def part_order():
    freq = np.arange(NF).reshape(2, 64, 1, 2)
    return np.concatenate([freq, freq + NF], axis=2).reshape(2 * NF)


def tables():
    angle = (np.arange(NT)[:, None] * np.arange(1, NF + 1)[None, :] % NT) * (2.0 * np.pi / NT)
    waves = np.concatenate([np.cos(angle), -np.sin(angle)], axis=1)[:, part_order()]
    forward = (waves / np.sqrt(NT)).astype(np.float32).astype(ml_dtypes.bfloat16)
    inverse = (waves * (2.0 / np.sqrt(NT))).astype(np.float32).astype(ml_dtypes.bfloat16)
    first = forward[: NT // 2]
    return np.ascontiguousarray(first.reshape(NT // 2, 2, 256).transpose(1, 0, 2)), np.ascontiguousarray(first.T), inverse


def one_hot(rows, depth):
    return np.eye(depth, dtype=np.float32)[np.asarray(rows).reshape(-1)].astype(ml_dtypes.bfloat16)


SHOT_MAJOR = one_hot(np.arange(256).reshape(64, 4).T, 256)
TIME_MAJOR = one_hot(np.arange(256).reshape(4, 64).T, 256)
PART_MAJOR = one_hot(np.arange(256).reshape(32, 2, 4).transpose(2, 1, 0), 256)
PART_SUM = (PART_MAJOR.reshape(4, 2, 32, 256)[:, 0] + PART_MAJOR.reshape(4, 2, 32, 256)[:, 1]).reshape(128, 256)
SPREAD = one_hot(np.broadcast_to(np.arange(128).reshape(4, 32).T[:, None, :], (32, 2, 4)), 128)
WIDE = NT // 4


def held(x):
    return pltpu.with_memory_space_constraint(x, pltpu.HBM)


def records_kernel(
    records_ref, table_ref, flipped_ref, aperture_ref, give_ref, keep_ref, picks_ref, piece_ref, rec, tab, ape, sems
):
    core = lax.axis_index("core")
    halves = (1 - core, core)
    lanes = [pl.ds(k * WIDE, WIDE) for k in (0, 2, 1, 3)]
    small = pltpu.make_async_copy(aperture_ref, ape, sems.at[4, 0])
    small.start()
    waits = []
    for k in range(4):
        waits.append([pltpu.make_async_copy(records_ref.at[0, :, :, lanes[k]], rec.at[k], sems.at[k, 2])])
        if k % 2 == 0:
            waits[k] += [
                pltpu.make_async_copy(table_ref.at[half, lanes[k]], tab.at[k // 2, i], sems.at[k, i])
                for i, half in enumerate(halves)
            ]
        for copy in waits[k]:
            copy.start()
    later = pltpu.make_async_copy(
        flipped_ref.at[pl.ds(pl.multiple_of(core * 256, 256), 256)], piece_ref, sems.at[4, 1]
    )
    later.start()
    c = lax.broadcasted_iota(jnp.int32, (64, 64), 0)
    j = lax.broadcasted_iota(jnp.int32, (64, 64), 1)
    order = (c == 2 * (j & 31) + (j >> 5)).astype(F32).astype(BF16)
    sign = (2 * (lax.broadcasted_iota(jnp.int32, (1, 256), 1) & 1) - 1).astype(F32).astype(BF16)
    small.wait()
    picks = jnp.dot(ape[...].reshape(4, 64).astype(F32).astype(BF16), order, preferred_element_type=F32).astype(BF16)
    picks_ref[...] = picks
    give_ref[256:272, :] = jnp.zeros((16, 512), BF16)
    give_ref[256:260, 0:64] = picks
    total = [None, None]
    for k in range(4):
        for copy in waits[k]:
            copy.wait()
        for i in range(2):
            waves = tab[k // 2, i]
            if k % 2 == 1:
                waves = waves * sign
            part = jnp.dot(rec[k].reshape(512, WIDE), waves, preferred_element_type=F32)
            total[i] = part if total[i] is None else total[i] + part
    give_ref[0:256, :] = total[0].T.astype(BF16)
    keep_ref[...] = total[1].T.astype(BF16)
    later.wait()


def transform_records(records, table, flipped, aperture):
    return pl.pallas_call(
        records_kernel,
        out_shape=(
            jax.ShapeDtypeStruct((272, 512), BF16),
            jax.ShapeDtypeStruct((256, 512), BF16),
            jax.ShapeDtypeStruct((4, 64), BF16),
            jax.ShapeDtypeStruct((256, 1024), BF16),
        ),
        in_specs=[ANY, ANY, ANY, ANY],
        out_specs=(VMEM, VMEM, VMEM, VMEM),
        scratch_shapes=[
            pltpu.VMEM((4, 2, 256, WIDE), BF16),
            pltpu.VMEM((2, 2, WIDE, 256), BF16),
            pltpu.VMEM((4, 1, 64), jnp.int32),
            pltpu.SemaphoreType.DMA((5, 3)),
        ],
        compiler_params=PARAMS,
        cost_estimate=pl.CostEstimate(flops=2**30, bytes_accessed=5 * 2**20, transcendentals=0),
        name="records",
    )(held(records), held(table), held(flipped), held(aperture))


def targets_kernel(own_ref, other_ref, piece_ref, keep_ref, order_ref, out_ref, flat):
    core = lax.axis_index("core")
    out_ref[:, :, 0:512] = keep_ref[...].reshape(64, 4, 512)
    total = None
    for i, raw_ref in enumerate((own_ref, other_ref)):
        for t in range(8):
            rows = jnp.dot(
                order_ref[...], raw_ref[64 * t : 64 * t + 64].reshape(256, 256), preferred_element_type=F32
            ).astype(BF16)
            for s in range(4):
                flat[i, 64 * t : 64 * t + 64, 256 * s : 256 * s + 256] = rows[64 * s : 64 * s + 64]
        at = core if i == 0 else 1 - core
        waves = piece_ref[:, pl.ds(pl.multiple_of(at * 512, 512), 512)]
        part = jnp.dot(waves, flat[i], preferred_element_type=F32)
        total = part if total is None else total + part
    odd = 1 - (lax.broadcasted_iota(jnp.int32, (256, 1), 0) & 1)
    total = total * (1 - 2 * odd * lax.axis_index("xh")).astype(F32)
    out_ref[:, :, 1024:2048] = total.astype(BF16).reshape(64, 4, 1024)


def transform_targets(own, other, piece, keep):
    return pl.pallas_call(
        targets_kernel,
        out_shape=jax.ShapeDtypeStruct((64, 4, 2176), BF16),
        in_specs=[VMEM, VMEM, VMEM, VMEM, VMEM],
        out_specs=VMEM,
        scratch_shapes=[pltpu.VMEM((2, 512, 1024), BF16)],
        compiler_params=PARAMS,
        cost_estimate=pl.CostEstimate(flops=2**30, bytes_accessed=4 * 2**20, transcendentals=0),
        name="targets",
    )(own, other, piece, keep, SHOT_MAJOR)


def fill_kernel(message_ref, taken_ref, picks_ref, out_ref, block, picks, sems):
    block[...] = taken_ref[0:256, :].reshape(64, 4, 512)
    both = jnp.concatenate([picks_ref[...], taken_ref[256:260, 0:64]], axis=1)
    picks[...] = jnp.broadcast_to(both[None], (64, 4, 128))
    first = pltpu.make_async_copy(block, out_ref.at[:, :, 512:1024], sems.at[0])
    second = pltpu.make_async_copy(picks, out_ref.at[:, :, 2048:2176], sems.at[1])
    first.start()
    second.start()
    first.wait()
    second.wait()


def fill(message, taken, picks):
    return pl.pallas_call(
        fill_kernel,
        out_shape=jax.ShapeDtypeStruct((64, 4, 2176), BF16),
        in_specs=[ANY, VMEM, VMEM],
        out_specs=ANY,
        scratch_shapes=[
            pltpu.VMEM((64, 4, 512), BF16),
            pltpu.VMEM((64, 4, 128), BF16),
            pltpu.SemaphoreType.DMA((2,)),
        ],
        input_output_aliases={0: 0},
        compiler_params=PARAMS,
        name="fill",
    )(message, taken, picks)


def lane_pick(low, high, index):
    inside = index & 127
    a = jnp.take_along_axis(low, inside, axis=1, mode="promise_in_bounds")
    b = jnp.take_along_axis(high, inside, axis=1, mode="promise_in_bounds")
    return jnp.where(index < 128, a, b)


def mix_kernel(got_ref, order_ref, both_ref, spread_ref, out_ref):
    order = order_ref[...]
    rows = jnp.dot(order, got_ref[:, :, 0:1024].reshape(256, 1024), preferred_element_type=F32).astype(BF16)
    shots = jnp.dot(both_ref[...], got_ref[:, :, 1024:2048].reshape(256, 1024), preferred_element_type=F32)
    where = jnp.dot(order, got_ref[:, :, 2048:2176].reshape(256, 128), preferred_element_type=F32).astype(jnp.int32)
    picks, gathers = [], []
    for p in range(4):
        parts = []
        for s in range(4):
            low = shots[32 * p : 32 * p + 32, 256 * s : 256 * s + 128]
            high = shots[32 * p : 32 * p + 32, 256 * s + 128 : 256 * s + 256]
            parts.append(
                jnp.concatenate(
                    [lane_pick(low, high, where[64 * s + 32 * h : 64 * s + 32 * h + 32]) for h in range(2)], axis=1
                )
            )
        picks.append(jnp.concatenate(parts, axis=0))
        gathers.append(
            jnp.concatenate(
                [
                    rows[64 * p + 32 * h : 64 * p + 32 * h + 32, 256 * b : 256 * b + 256]
                    for h in range(2)
                    for b in range(4)
                ],
                axis=0,
            )
        )
    total = [None] * 4
    for f in range(2):
        re, im, minus = picks[f].astype(BF16), picks[2 + f].astype(BF16), (-picks[2 + f]).astype(BF16)
        left = jnp.concatenate(
            [jnp.concatenate([re, minus], axis=1), jnp.concatenate([im, re], axis=1)], axis=0
        )
        right = jnp.concatenate([gathers[f], gathers[2 + f]], axis=0)
        out = jnp.dot(left, right, preferred_element_type=F32).astype(BF16)
        for part in range(2):
            total[2 * part + f] = jnp.concatenate(
                [out[128 * part + 32 * s : 128 * part + 32 * s + 32] for s in range(4)], axis=1
            )
    total = jnp.concatenate(total, axis=0)
    out_ref[...] = (
        jnp.dot(spread_ref[...], total, preferred_element_type=F32).astype(BF16).reshape(64, 4, 1024)
    )


def mix(got):
    return pl.pallas_call(
        mix_kernel,
        out_shape=jax.ShapeDtypeStruct((64, 4, 1024), BF16),
        in_specs=[VMEM, VMEM, VMEM, VMEM],
        out_specs=VMEM,
        compiler_params=PARAMS,
        name="mix",
    )(got, PART_MAJOR, PART_SUM, SPREAD)


def inverse_waves(table_ref, half, rows, count):
    block = 2 * lax.axis_index("xh") + lax.axis_index("core")
    return table_ref[
        pl.ds(pl.multiple_of(block * 512 + rows, 256), count), pl.ds(pl.multiple_of(half * 256, 256), 256)
    ]


def own_half_kernel(own_ref, table_ref, out_ref):
    waves = inverse_waves(table_ref, lax.axis_index("core"), 0, 512)
    out_ref[...] = jnp.dot(waves, own_ref[...].reshape(256, 1024), preferred_element_type=F32)


def own_half(own, table):
    return pl.pallas_call(
        own_half_kernel,
        out_shape=jax.ShapeDtypeStruct((512, 1024), F32),
        in_specs=[VMEM, VMEM],
        out_specs=VMEM,
        compiler_params=PARAMS,
        cost_estimate=pl.CostEstimate(flops=2**28, bytes_accessed=2**20, transcendentals=0),
        name="own_half",
    )(own, table)


def inverse_kernel(part_ref, other_ref, table_ref, order_ref, out_ref, ready, sems):
    other = other_ref[...].reshape(256, 1024)
    outs = []
    for half in range(2):
        waves = inverse_waves(table_ref, 1 - lax.axis_index("core"), 256 * half, 256)
        here = jnp.dot(waves, other, preferred_element_type=F32)
        here = (here + part_ref[256 * half : 256 * half + 256]).astype(BF16)
        for t in range(4):
            at = 256 * half + 64 * t
            stack = jnp.concatenate(
                [here[64 * t : 64 * t + 64, 256 * s : 256 * s + 256] for s in range(4)], axis=0
            )
            ready[at : at + 64] = (
                jnp.dot(order_ref[...], stack, preferred_element_type=F32).astype(BF16).reshape(64, 4, 256)
            )
            if t >= 0:
                rows = pl.ds(at, 64)
                outs.append(pltpu.make_async_copy(ready.at[rows], out_ref.at[rows], sems.at[len(outs)]))
                outs[-1].start()
    for copy in outs:
        copy.wait()


def transform_back(part, other, table):
    return pl.pallas_call(
        inverse_kernel,
        out_shape=jax.ShapeDtypeStruct((512, 4, 256), BF16),
        in_specs=[VMEM, VMEM, VMEM, VMEM],
        out_specs=ANY,
        scratch_shapes=[pltpu.VMEM((512, 4, 256), BF16), pltpu.SemaphoreType.DMA((8,))],
        compiler_params=PARAMS,
        name="inverse",
    )(part, other, table, TIME_MAJOR)


def on_device(records, targets, aperture):
    forward, flipped, inverse = tables()
    swap = [(0, 1), (1, 0)]
    others = lax.ppermute(targets, "core", swap)
    give, keep, picks, piece = transform_records(records, forward, flipped, aperture)
    taken = lax.ppermute(give, "core", swap)
    message = transform_targets(targets, others, piece, keep)
    message = fill(message, taken, picks)
    got = lax.all_to_all(message, ("shot", "xh"), 0, 0, tiled=True)
    back = lax.all_to_all(mix(got), ("shot", "xh"), 0, 0, tiled=True)
    other = lax.ppermute(back, "core", swap)
    return transform_back(own_half(back, inverse), other, inverse)


def solution(mesh):
    cut = Mesh(mesh.devices.reshape(32, 2, 2), ("shot", "xh", "core"))
    xline = ("xh", "core")
    return jax.shard_map(
        on_device,
        mesh=cut,
        in_specs=(P(xline, "shot", None, None), P(xline, "shot", None), P("shot", xline, None)),
        out_specs=P(xline, "shot", None),
        check_vma=False,
    )
```

```python
import jax
import jax.numpy as jnp
import ml_dtypes
import numpy as np
from jax import lax
from jax.experimental import pallas as pl
from jax.experimental.pallas import tpu as pltpu
from jax.sharding import Mesh, PartitionSpec as P

NT = 2048
NF = 256
BF16 = jnp.bfloat16
F32 = jnp.float32
VMEM = pl.BlockSpec(memory_space=pltpu.VMEM)
ANY = pl.BlockSpec(memory_space=pl.ANY)
PARAMS = pltpu.CompilerParams(vmem_limit_bytes=24 * 2**20)


def part_order():
    freq = np.arange(NF).reshape(2, 64, 1, 2)
    return np.concatenate([freq, freq + NF], axis=2).reshape(2 * NF)


def tables():
    angle = (np.arange(NT)[:, None] * np.arange(1, NF + 1)[None, :] % NT) * (2.0 * np.pi / NT)
    waves = np.concatenate([np.cos(angle), -np.sin(angle)], axis=1)[:, part_order()]
    forward = (waves / np.sqrt(NT)).astype(np.float32).astype(ml_dtypes.bfloat16)
    inverse = (waves * (2.0 / np.sqrt(NT))).astype(np.float32).astype(ml_dtypes.bfloat16)
    first = forward[: NT // 2]
    return np.ascontiguousarray(first.reshape(NT // 2, 2, 256).transpose(1, 0, 2)), np.ascontiguousarray(first.T), inverse


def one_hot(rows, depth):
    return np.eye(depth, dtype=np.float32)[np.asarray(rows).reshape(-1)].astype(ml_dtypes.bfloat16)


SHOT_MAJOR = one_hot(np.arange(256).reshape(64, 4).T, 256)
TIME_MAJOR = one_hot(np.arange(256).reshape(4, 64).T, 256)
PART_MAJOR = one_hot(np.arange(256).reshape(32, 2, 4).transpose(2, 1, 0), 256)
PART_SUM = (PART_MAJOR.reshape(4, 2, 32, 256)[:, 0] + PART_MAJOR.reshape(4, 2, 32, 256)[:, 1]).reshape(128, 256)
SPREAD = one_hot(np.broadcast_to(np.arange(128).reshape(4, 32).T[:, None, :], (32, 2, 4)), 128)
WIDE = NT // 4


def held(x):
    return pltpu.with_memory_space_constraint(x, pltpu.HBM)


def bin_sign():
    return (2 * (lax.broadcasted_iota(jnp.int32, (1, 256), 1) & 1) - 1).astype(F32).astype(BF16)


def record_spectra(rec, waves):
    total = None
    for k in range(4):
        wave = waves[WIDE * (k % 2) : WIDE * (k % 2) + WIDE]
        wave = wave if k < 2 else wave * bin_sign()
        part = jnp.dot(rec[:, :, WIDE * k : WIDE * k + WIDE].reshape(512, WIDE), wave, preferred_element_type=F32)
        total = part if total is None else total + part
    return total.T.astype(BF16)


def give_kernel(
    records_ref, table_ref, flipped_ref, aperture_ref, give_ref, picks_ref, rec, keep, piece_ref, tab, ape, sems
):
    core = lax.axis_index("core")
    small = pltpu.make_async_copy(aperture_ref, ape, sems.at[5])
    small.start()
    first = [pltpu.make_async_copy(table_ref.at[1 - core], tab, sems.at[0])]
    for c in range(2):
        first.append(pltpu.make_async_copy(records_ref.at[0, c], rec.at[c], sems.at[1 + c]))
    later = [
        pltpu.make_async_copy(table_ref.at[core], keep, sems.at[3]),
        pltpu.make_async_copy(flipped_ref.at[pl.ds(pl.multiple_of(core * 256, 256), 256)], piece_ref, sems.at[4]),
    ]
    for copy in first + later:
        copy.start()
    c = lax.broadcasted_iota(jnp.int32, (64, 64), 0)
    j = lax.broadcasted_iota(jnp.int32, (64, 64), 1)
    order = (c == 2 * (j & 31) + (j >> 5)).astype(F32).astype(BF16)
    small.wait()
    picks = jnp.dot(ape[...].reshape(4, 64).astype(F32).astype(BF16), order, preferred_element_type=F32).astype(BF16)
    picks_ref[...] = picks
    give_ref[256:272, :] = jnp.zeros((16, 512), BF16)
    give_ref[256:260, 0:64] = picks
    for copy in first:
        copy.wait()
    give_ref[0:256, :] = record_spectra(rec, tab)
    for copy in later:
        copy.wait()


def transform_given(records, table, flipped, aperture):
    return pl.pallas_call(
        give_kernel,
        out_shape=(
            jax.ShapeDtypeStruct((272, 512), BF16),
            jax.ShapeDtypeStruct((4, 64), BF16),
            jax.ShapeDtypeStruct((2, 256, NT), BF16),
            jax.ShapeDtypeStruct((NT // 2, 256), BF16),
            jax.ShapeDtypeStruct((256, 1024), BF16),
        ),
        in_specs=[ANY, ANY, ANY, ANY],
        out_specs=(VMEM, VMEM, VMEM, VMEM, VMEM),
        scratch_shapes=[
            pltpu.VMEM((NT // 2, 256), BF16),
            pltpu.VMEM((4, 1, 64), jnp.int32),
            pltpu.SemaphoreType.DMA((6,)),
        ],
        compiler_params=PARAMS,
        cost_estimate=pl.CostEstimate(flops=2**29, bytes_accessed=5 * 2**20, transcendentals=0),
        name="give",
    )(held(records), held(table), held(flipped), held(aperture))


def keep_kernel(rec_ref, keep_ref, own_ref, other_ref, piece_ref, order_ref, out_ref, flat):
    core = lax.axis_index("core")
    out_ref[:, :, 0:512] = record_spectra(rec_ref, keep_ref).reshape(64, 4, 512)
    total = None
    for i, raw_ref in enumerate((own_ref, other_ref)):
        for t in range(8):
            rows = jnp.dot(
                order_ref[...], raw_ref[64 * t : 64 * t + 64].reshape(256, 256), preferred_element_type=F32
            ).astype(BF16)
            for s in range(4):
                flat[i, 64 * t : 64 * t + 64, 256 * s : 256 * s + 256] = rows[64 * s : 64 * s + 64]
        at = core if i == 0 else 1 - core
        waves = piece_ref[:, pl.ds(pl.multiple_of(at * 512, 512), 512)]
        part = jnp.dot(waves, flat[i], preferred_element_type=F32)
        total = part if total is None else total + part
    odd = 1 - (lax.broadcasted_iota(jnp.int32, (256, 1), 0) & 1)
    total = total * (1 - 2 * odd * lax.axis_index("xh")).astype(F32)
    out_ref[:, :, 1024:2048] = total.astype(BF16).reshape(64, 4, 1024)


def transform_kept(rec, keep, own, other, piece):
    return pl.pallas_call(
        keep_kernel,
        out_shape=jax.ShapeDtypeStruct((64, 4, 2176), BF16),
        in_specs=[VMEM] * 6,
        out_specs=VMEM,
        scratch_shapes=[pltpu.VMEM((2, 512, 1024), BF16)],
        compiler_params=PARAMS,
        cost_estimate=pl.CostEstimate(flops=3 * 2**29, bytes_accessed=4 * 2**20, transcendentals=0),
        name="keep",
    )(rec, keep, own, other, piece, SHOT_MAJOR)


def fill_kernel(message_ref, taken_ref, picks_ref, out_ref, block, picks, sems):
    block[...] = taken_ref[0:256, :].reshape(64, 4, 512)
    both = jnp.concatenate([picks_ref[...], taken_ref[256:260, 0:64]], axis=1)
    picks[...] = jnp.broadcast_to(both[None], (64, 4, 128))
    first = pltpu.make_async_copy(block, out_ref.at[:, :, 512:1024], sems.at[0])
    second = pltpu.make_async_copy(picks, out_ref.at[:, :, 2048:2176], sems.at[1])
    first.start()
    second.start()
    first.wait()
    second.wait()


def fill(message, taken, picks):
    return pl.pallas_call(
        fill_kernel,
        out_shape=jax.ShapeDtypeStruct((64, 4, 2176), BF16),
        in_specs=[ANY, VMEM, VMEM],
        out_specs=ANY,
        scratch_shapes=[
            pltpu.VMEM((64, 4, 512), BF16),
            pltpu.VMEM((64, 4, 128), BF16),
            pltpu.SemaphoreType.DMA((2,)),
        ],
        input_output_aliases={0: 0},
        compiler_params=PARAMS,
        name="fill",
    )(message, taken, picks)


def lane_pick(low, high, index):
    inside = index & 127
    a = jnp.take_along_axis(low, inside, axis=1, mode="promise_in_bounds")
    b = jnp.take_along_axis(high, inside, axis=1, mode="promise_in_bounds")
    return jnp.where(index < 128, a, b)


def mix_kernel(got_ref, order_ref, both_ref, spread_ref, out_ref):
    order = order_ref[...]
    rows = jnp.dot(order, got_ref[:, :, 0:1024].reshape(256, 1024), preferred_element_type=F32).astype(BF16)
    shots = jnp.dot(both_ref[...], got_ref[:, :, 1024:2048].reshape(256, 1024), preferred_element_type=F32)
    where = jnp.dot(order, got_ref[:, :, 2048:2176].reshape(256, 128), preferred_element_type=F32).astype(jnp.int32)
    picks, gathers = [], []
    for p in range(4):
        parts = []
        for s in range(4):
            low = shots[32 * p : 32 * p + 32, 256 * s : 256 * s + 128]
            high = shots[32 * p : 32 * p + 32, 256 * s + 128 : 256 * s + 256]
            parts.append(
                jnp.concatenate(
                    [lane_pick(low, high, where[64 * s + 32 * h : 64 * s + 32 * h + 32]) for h in range(2)], axis=1
                )
            )
        picks.append(jnp.concatenate(parts, axis=0))
        gathers.append(
            jnp.concatenate(
                [
                    rows[64 * p + 32 * h : 64 * p + 32 * h + 32, 256 * b : 256 * b + 256]
                    for h in range(2)
                    for b in range(4)
                ],
                axis=0,
            )
        )
    total = [None] * 4
    for f in range(2):
        re, im, minus = picks[f].astype(BF16), picks[2 + f].astype(BF16), (-picks[2 + f]).astype(BF16)
        left = jnp.concatenate(
            [jnp.concatenate([re, minus], axis=1), jnp.concatenate([im, re], axis=1)], axis=0
        )
        right = jnp.concatenate([gathers[f], gathers[2 + f]], axis=0)
        out = jnp.dot(left, right, preferred_element_type=F32).astype(BF16)
        for part in range(2):
            total[2 * part + f] = jnp.concatenate(
                [out[128 * part + 32 * s : 128 * part + 32 * s + 32] for s in range(4)], axis=1
            )
    total = jnp.concatenate(total, axis=0)
    out_ref[...] = (
        jnp.dot(spread_ref[...], total, preferred_element_type=F32).astype(BF16).reshape(64, 4, 1024)
    )


def mix(got):
    return pl.pallas_call(
        mix_kernel,
        out_shape=jax.ShapeDtypeStruct((64, 4, 1024), BF16),
        in_specs=[VMEM, VMEM, VMEM, VMEM],
        out_specs=VMEM,
        compiler_params=PARAMS,
        name="mix",
    )(got, PART_MAJOR, PART_SUM, SPREAD)


def inverse_waves(table_ref, half, rows, count):
    block = 2 * lax.axis_index("xh") + lax.axis_index("core")
    return table_ref[
        pl.ds(pl.multiple_of(block * 512 + rows, 256), count), pl.ds(pl.multiple_of(half * 256, 256), 256)
    ]


def own_half_kernel(own_ref, table_ref, out_ref):
    waves = inverse_waves(table_ref, lax.axis_index("core"), 0, 512)
    out_ref[...] = jnp.dot(waves, own_ref[...].reshape(256, 1024), preferred_element_type=F32)


def own_half(own, table):
    return pl.pallas_call(
        own_half_kernel,
        out_shape=jax.ShapeDtypeStruct((512, 1024), F32),
        in_specs=[VMEM, VMEM],
        out_specs=VMEM,
        compiler_params=PARAMS,
        cost_estimate=pl.CostEstimate(flops=2**28, bytes_accessed=2**20, transcendentals=0),
        name="own_half",
    )(own, table)


def inverse_kernel(part_ref, other_ref, table_ref, order_ref, out_ref, ready, sems):
    other = other_ref[...].reshape(256, 1024)
    outs = []
    for half in range(2):
        waves = inverse_waves(table_ref, 1 - lax.axis_index("core"), 256 * half, 256)
        here = jnp.dot(waves, other, preferred_element_type=F32)
        here = (here + part_ref[256 * half : 256 * half + 256]).astype(BF16)
        for t in range(4):
            at = 256 * half + 64 * t
            stack = jnp.concatenate(
                [here[64 * t : 64 * t + 64, 256 * s : 256 * s + 256] for s in range(4)], axis=0
            )
            ready[at : at + 64] = (
                jnp.dot(order_ref[...], stack, preferred_element_type=F32).astype(BF16).reshape(64, 4, 256)
            )
            if t >= 0:
                rows = pl.ds(at, 64)
                outs.append(pltpu.make_async_copy(ready.at[rows], out_ref.at[rows], sems.at[len(outs)]))
                outs[-1].start()
    for copy in outs:
        copy.wait()


def transform_back(part, other, table):
    return pl.pallas_call(
        inverse_kernel,
        out_shape=jax.ShapeDtypeStruct((512, 4, 256), BF16),
        in_specs=[VMEM, VMEM, VMEM, VMEM],
        out_specs=ANY,
        scratch_shapes=[pltpu.VMEM((512, 4, 256), BF16), pltpu.SemaphoreType.DMA((8,))],
        compiler_params=PARAMS,
        name="inverse",
    )(part, other, table, TIME_MAJOR)


def on_device(records, targets, aperture):
    forward, flipped, inverse = tables()
    swap = [(0, 1), (1, 0)]
    others = lax.ppermute(targets, "core", swap)
    give, picks, rec, keep, piece = transform_given(records, forward, flipped, aperture)
    taken = lax.ppermute(give, "core", swap)
    message = transform_kept(rec, keep, targets, others, piece)
    message = fill(message, taken, picks)
    got = lax.all_to_all(message, ("shot", "xh"), 0, 0, tiled=True)
    back = lax.all_to_all(mix(got), ("shot", "xh"), 0, 0, tiled=True)
    other = lax.ppermute(back, "core", swap)
    return transform_back(own_half(back, inverse), other, inverse)


def solution(mesh):
    cut = Mesh(mesh.devices.reshape(32, 2, 2), ("shot", "xh", "core"))
    xline = ("xh", "core")
    return jax.shard_map(
        on_device,
        mesh=cut,
        in_specs=(P(xline, "shot", None, None), P(xline, "shot", None), P("shot", xline, None)),
        out_specs=P(xline, "shot", None),
        check_vma=False,
    )
```

```python
import jax
import jax.numpy as jnp
import ml_dtypes
import numpy as np
from jax import lax
from jax.experimental import pallas as pl
from jax.experimental.pallas import tpu as pltpu
from jax.sharding import Mesh, PartitionSpec as P

NT = 2048
NF = 256
BF16 = jnp.bfloat16
F32 = jnp.float32
VMEM = pl.BlockSpec(memory_space=pltpu.VMEM)
ANY = pl.BlockSpec(memory_space=pl.ANY)
PARAMS = pltpu.CompilerParams(vmem_limit_bytes=24 * 2**20)


def part_order():
    freq = np.arange(NF).reshape(2, 64, 1, 2)
    return np.concatenate([freq, freq + NF], axis=2).reshape(2 * NF)


def tables():
    angle = (np.arange(NT)[:, None] * np.arange(1, NF + 1)[None, :] % NT) * (2.0 * np.pi / NT)
    waves = np.concatenate([np.cos(angle), -np.sin(angle)], axis=1)[:, part_order()]
    forward = (waves / np.sqrt(NT)).astype(np.float32).astype(ml_dtypes.bfloat16)
    inverse = (waves * (2.0 / np.sqrt(NT))).astype(np.float32).astype(ml_dtypes.bfloat16)
    first = forward[: NT // 2]
    return np.ascontiguousarray(first.reshape(NT // 2, 2, 256).transpose(1, 0, 2)), np.ascontiguousarray(first.T), inverse


def one_hot(rows, depth):
    return np.eye(depth, dtype=np.float32)[np.asarray(rows).reshape(-1)].astype(ml_dtypes.bfloat16)


SHOT_MAJOR = one_hot(np.arange(256).reshape(64, 4).T, 256)
TIME_MAJOR = one_hot(np.arange(256).reshape(4, 64).T, 256)
TURN = 2


def chip_order():
    order = []
    for a in range(64):
        z, y, x = (a // 16 + TURN) % 4, (a // 4 + TURN) % 4, (a + TURN) % 4
        order.append(((4 * z + y) * 2 + x % 2, x // 2))
    return order


CHIPS = chip_order()
RANK = np.zeros((32, 2), np.int64)
for rank, chip in enumerate(CHIPS):
    RANK[chip] = rank
GROUPS = [[(2 * shot + high) * 2 + core for shot, high in CHIPS] for core in range(2)]
PART_MAJOR = one_hot(4 * RANK.T[None] + np.arange(4)[:, None, None], 256)
PART_SUM = (PART_MAJOR.reshape(4, 2, 32, 256)[:, 0] + PART_MAJOR.reshape(4, 2, 32, 256)[:, 1]).reshape(128, 256)
SPREAD = one_hot([[32 * o + shot for o in range(4)] for shot, _ in CHIPS], 128)


def exchange(x):
    return lax.all_to_all(x, ("shot", "xh", "core"), 0, 0, axis_index_groups=GROUPS, tiled=True)


WIDE = NT // 4


def held(x):
    return pltpu.with_memory_space_constraint(x, pltpu.HBM)


def bin_sign():
    return (2 * (lax.broadcasted_iota(jnp.int32, (1, 256), 1) & 1) - 1).astype(F32).astype(BF16)


def record_spectra(rec, waves):
    total = None
    for k in range(4):
        wave = waves[WIDE * (k % 2) : WIDE * (k % 2) + WIDE]
        wave = wave if k < 2 else wave * bin_sign()
        part = jnp.dot(rec[:, :, WIDE * k : WIDE * k + WIDE].reshape(512, WIDE), wave, preferred_element_type=F32)
        total = part if total is None else total + part
    return total.T.astype(BF16)


def give_kernel(
    records_ref, table_ref, flipped_ref, aperture_ref, give_ref, picks_ref, rec, keep, piece_ref, tab, ape, sems
):
    core = lax.axis_index("core")
    small = pltpu.make_async_copy(aperture_ref, ape, sems.at[5])
    small.start()
    first = [pltpu.make_async_copy(table_ref.at[1 - core], tab, sems.at[0])]
    for c in range(2):
        first.append(pltpu.make_async_copy(records_ref.at[0, c], rec.at[c], sems.at[1 + c]))
    later = [
        pltpu.make_async_copy(table_ref.at[core], keep, sems.at[3]),
        pltpu.make_async_copy(flipped_ref.at[pl.ds(pl.multiple_of(core * 256, 256), 256)], piece_ref, sems.at[4]),
    ]
    for copy in first + later:
        copy.start()
    c = lax.broadcasted_iota(jnp.int32, (64, 64), 0)
    j = lax.broadcasted_iota(jnp.int32, (64, 64), 1)
    order = (c == 2 * (j & 31) + (j >> 5)).astype(F32).astype(BF16)
    small.wait()
    picks = jnp.dot(ape[...].reshape(4, 64).astype(F32).astype(BF16), order, preferred_element_type=F32).astype(BF16)
    picks_ref[...] = picks
    give_ref[256:272, :] = jnp.zeros((16, 512), BF16)
    give_ref[256:260, 0:64] = picks
    for copy in first:
        copy.wait()
    give_ref[0:256, :] = record_spectra(rec, tab)
    for copy in later:
        copy.wait()


def transform_given(records, table, flipped, aperture):
    return pl.pallas_call(
        give_kernel,
        out_shape=(
            jax.ShapeDtypeStruct((272, 512), BF16),
            jax.ShapeDtypeStruct((4, 64), BF16),
            jax.ShapeDtypeStruct((2, 256, NT), BF16),
            jax.ShapeDtypeStruct((NT // 2, 256), BF16),
            jax.ShapeDtypeStruct((256, 1024), BF16),
        ),
        in_specs=[ANY, ANY, ANY, ANY],
        out_specs=(VMEM, VMEM, VMEM, VMEM, VMEM),
        scratch_shapes=[
            pltpu.VMEM((NT // 2, 256), BF16),
            pltpu.VMEM((4, 1, 64), jnp.int32),
            pltpu.SemaphoreType.DMA((6,)),
        ],
        compiler_params=PARAMS,
        cost_estimate=pl.CostEstimate(flops=2**29, bytes_accessed=5 * 2**20, transcendentals=0),
        name="give",
    )(held(records), held(table), held(flipped), held(aperture))


def keep_kernel(rec_ref, keep_ref, own_ref, other_ref, piece_ref, order_ref, out_ref, flat):
    core = lax.axis_index("core")
    out_ref[:, :, 0:512] = record_spectra(rec_ref, keep_ref).reshape(64, 4, 512)
    total = None
    for i, raw_ref in enumerate((own_ref, other_ref)):
        for t in range(8):
            rows = jnp.dot(
                order_ref[...], raw_ref[64 * t : 64 * t + 64].reshape(256, 256), preferred_element_type=F32
            ).astype(BF16)
            for s in range(4):
                flat[i, 64 * t : 64 * t + 64, 256 * s : 256 * s + 256] = rows[64 * s : 64 * s + 64]
        at = core if i == 0 else 1 - core
        waves = piece_ref[:, pl.ds(pl.multiple_of(at * 512, 512), 512)]
        part = jnp.dot(waves, flat[i], preferred_element_type=F32)
        total = part if total is None else total + part
    odd = 1 - (lax.broadcasted_iota(jnp.int32, (256, 1), 0) & 1)
    total = total * (1 - 2 * odd * lax.axis_index("xh")).astype(F32)
    out_ref[:, :, 1024:2048] = total.astype(BF16).reshape(64, 4, 1024)


def transform_kept(rec, keep, own, other, piece):
    return pl.pallas_call(
        keep_kernel,
        out_shape=jax.ShapeDtypeStruct((64, 4, 2176), BF16),
        in_specs=[VMEM] * 6,
        out_specs=VMEM,
        scratch_shapes=[pltpu.VMEM((2, 512, 1024), BF16)],
        compiler_params=PARAMS,
        cost_estimate=pl.CostEstimate(flops=3 * 2**29, bytes_accessed=4 * 2**20, transcendentals=0),
        name="keep",
    )(rec, keep, own, other, piece, SHOT_MAJOR)


def fill_kernel(message_ref, taken_ref, picks_ref, out_ref, block, picks, sems):
    block[...] = taken_ref[0:256, :].reshape(64, 4, 512)
    both = jnp.concatenate([picks_ref[...], taken_ref[256:260, 0:64]], axis=1)
    picks[...] = jnp.broadcast_to(both[None], (64, 4, 128))
    first = pltpu.make_async_copy(block, out_ref.at[:, :, 512:1024], sems.at[0])
    second = pltpu.make_async_copy(picks, out_ref.at[:, :, 2048:2176], sems.at[1])
    first.start()
    second.start()
    first.wait()
    second.wait()


def fill(message, taken, picks):
    return pl.pallas_call(
        fill_kernel,
        out_shape=jax.ShapeDtypeStruct((64, 4, 2176), BF16),
        in_specs=[ANY, VMEM, VMEM],
        out_specs=ANY,
        scratch_shapes=[
            pltpu.VMEM((64, 4, 512), BF16),
            pltpu.VMEM((64, 4, 128), BF16),
            pltpu.SemaphoreType.DMA((2,)),
        ],
        input_output_aliases={0: 0},
        compiler_params=PARAMS,
        name="fill",
    )(message, taken, picks)


def lane_pick(low, high, index):
    inside = index & 127
    a = jnp.take_along_axis(low, inside, axis=1, mode="promise_in_bounds")
    b = jnp.take_along_axis(high, inside, axis=1, mode="promise_in_bounds")
    return jnp.where(index < 128, a, b)


def mix_kernel(got_ref, order_ref, both_ref, spread_ref, out_ref):
    order = order_ref[...]
    rows = jnp.dot(order, got_ref[:, :, 0:1024].reshape(256, 1024), preferred_element_type=F32).astype(BF16)
    shots = jnp.dot(both_ref[...], got_ref[:, :, 1024:2048].reshape(256, 1024), preferred_element_type=F32)
    where = jnp.dot(order, got_ref[:, :, 2048:2176].reshape(256, 128), preferred_element_type=F32).astype(jnp.int32)
    picks, gathers = [], []
    for p in range(4):
        parts = []
        for s in range(4):
            low = shots[32 * p : 32 * p + 32, 256 * s : 256 * s + 128]
            high = shots[32 * p : 32 * p + 32, 256 * s + 128 : 256 * s + 256]
            parts.append(
                jnp.concatenate(
                    [lane_pick(low, high, where[64 * s + 32 * h : 64 * s + 32 * h + 32]) for h in range(2)], axis=1
                )
            )
        picks.append(jnp.concatenate(parts, axis=0))
        gathers.append(
            jnp.concatenate(
                [
                    rows[64 * p + 32 * h : 64 * p + 32 * h + 32, 256 * b : 256 * b + 256]
                    for h in range(2)
                    for b in range(4)
                ],
                axis=0,
            )
        )
    total = [None] * 4
    for f in range(2):
        re, im, minus = picks[f].astype(BF16), picks[2 + f].astype(BF16), (-picks[2 + f]).astype(BF16)
        left = jnp.concatenate(
            [jnp.concatenate([re, minus], axis=1), jnp.concatenate([im, re], axis=1)], axis=0
        )
        right = jnp.concatenate([gathers[f], gathers[2 + f]], axis=0)
        out = jnp.dot(left, right, preferred_element_type=F32).astype(BF16)
        for part in range(2):
            total[2 * part + f] = jnp.concatenate(
                [out[128 * part + 32 * s : 128 * part + 32 * s + 32] for s in range(4)], axis=1
            )
    total = jnp.concatenate(total, axis=0)
    out_ref[...] = (
        jnp.dot(spread_ref[...], total, preferred_element_type=F32).astype(BF16).reshape(64, 4, 1024)
    )


def mix(got):
    return pl.pallas_call(
        mix_kernel,
        out_shape=jax.ShapeDtypeStruct((64, 4, 1024), BF16),
        in_specs=[VMEM, VMEM, VMEM, VMEM],
        out_specs=VMEM,
        compiler_params=PARAMS,
        name="mix",
    )(got, PART_MAJOR, PART_SUM, SPREAD)


def inverse_waves(table_ref, half, rows, count):
    block = 2 * lax.axis_index("xh") + lax.axis_index("core")
    return table_ref[
        pl.ds(pl.multiple_of(block * 512 + rows, 256), count), pl.ds(pl.multiple_of(half * 256, 256), 256)
    ]


def own_half_kernel(own_ref, table_ref, out_ref):
    waves = inverse_waves(table_ref, lax.axis_index("core"), 0, 512)
    out_ref[...] = jnp.dot(waves, own_ref[...].reshape(256, 1024), preferred_element_type=F32)


def own_half(own, table):
    return pl.pallas_call(
        own_half_kernel,
        out_shape=jax.ShapeDtypeStruct((512, 1024), F32),
        in_specs=[VMEM, VMEM],
        out_specs=VMEM,
        compiler_params=PARAMS,
        cost_estimate=pl.CostEstimate(flops=2**28, bytes_accessed=2**20, transcendentals=0),
        name="own_half",
    )(own, table)


def inverse_kernel(part_ref, other_ref, table_ref, order_ref, out_ref, ready, sems):
    other = other_ref[...].reshape(256, 1024)
    outs = []
    for half in range(2):
        waves = inverse_waves(table_ref, 1 - lax.axis_index("core"), 256 * half, 256)
        here = jnp.dot(waves, other, preferred_element_type=F32)
        here = (here + part_ref[256 * half : 256 * half + 256]).astype(BF16)
        for t in range(4):
            at = 256 * half + 64 * t
            stack = jnp.concatenate(
                [here[64 * t : 64 * t + 64, 256 * s : 256 * s + 256] for s in range(4)], axis=0
            )
            ready[at : at + 64] = (
                jnp.dot(order_ref[...], stack, preferred_element_type=F32).astype(BF16).reshape(64, 4, 256)
            )
            if t >= 0:
                rows = pl.ds(at, 64)
                outs.append(pltpu.make_async_copy(ready.at[rows], out_ref.at[rows], sems.at[len(outs)]))
                outs[-1].start()
    for copy in outs:
        copy.wait()


def transform_back(part, other, table):
    return pl.pallas_call(
        inverse_kernel,
        out_shape=jax.ShapeDtypeStruct((512, 4, 256), BF16),
        in_specs=[VMEM, VMEM, VMEM, VMEM],
        out_specs=ANY,
        scratch_shapes=[pltpu.VMEM((512, 4, 256), BF16), pltpu.SemaphoreType.DMA((8,))],
        compiler_params=PARAMS,
        name="inverse",
    )(part, other, table, TIME_MAJOR)


def on_device(records, targets, aperture):
    forward, flipped, inverse = tables()
    swap = [(0, 1), (1, 0)]
    others = lax.ppermute(targets, "core", swap)
    give, picks, rec, keep, piece = transform_given(records, forward, flipped, aperture)
    taken = lax.ppermute(give, "core", swap)
    message = transform_kept(rec, keep, targets, others, piece)
    message = fill(message, taken, picks)
    back = exchange(mix(exchange(message)))
    other = lax.ppermute(back, "core", swap)
    return transform_back(own_half(back, inverse), other, inverse)


def solution(mesh):
    cut = Mesh(mesh.devices.reshape(32, 2, 2), ("shot", "xh", "core"))
    xline = ("xh", "core")
    return jax.shard_map(
        on_device,
        mesh=cut,
        in_specs=(P(xline, "shot", None, None), P(xline, "shot", None), P("shot", xline, None)),
        out_specs=P(xline, "shot", None),
        check_vma=False,
    )
```

```python
import jax
import jax.numpy as jnp
import ml_dtypes
import numpy as np
from jax import lax
from jax.experimental import pallas as pl
from jax.experimental.pallas import tpu as pltpu
from jax.sharding import Mesh, PartitionSpec as P

NT = 2048
NF = 256
BF16 = jnp.bfloat16
F32 = jnp.float32
VMEM = pl.BlockSpec(memory_space=pltpu.VMEM)
ANY = pl.BlockSpec(memory_space=pl.ANY)
PARAMS = pltpu.CompilerParams(vmem_limit_bytes=24 * 2**20)


def part_order():
    freq = np.arange(NF).reshape(2, 64, 1, 2)
    return np.concatenate([freq, freq + NF], axis=2).reshape(2 * NF)


def tables():
    angle = (np.arange(NT)[:, None] * np.arange(1, NF + 1)[None, :] % NT) * (2.0 * np.pi / NT)
    waves = np.concatenate([np.cos(angle), -np.sin(angle)], axis=1)[:, part_order()]
    forward = (waves / np.sqrt(NT)).astype(np.float32).astype(ml_dtypes.bfloat16)
    returned = np.concatenate([RETURNED, 256 + RETURNED])
    inverse = (waves[:, returned] * (2.0 / np.sqrt(NT))).astype(np.float32).astype(ml_dtypes.bfloat16)
    first = forward[: NT // 2]
    return np.ascontiguousarray(first.reshape(NT // 2, 2, 256).transpose(1, 0, 2)), np.ascontiguousarray(first.T), inverse


def one_hot(rows, depth):
    return np.eye(depth, dtype=np.float32)[np.asarray(rows).reshape(-1)].astype(ml_dtypes.bfloat16)


SHOT_MAJOR = one_hot(np.arange(256).reshape(64, 4).T, 256)
TIME_MAJOR = one_hot(np.arange(256).reshape(4, 64).T, 256)
def chip_order(turn, sign, axes=(0, 1, 2), stride=1):
    order = []
    for a in range(64):
        a = a * stride % 64
        at = [0, 0, 0]
        for axis, digit in zip(axes, (a // 16, a // 4 % 4, a % 4)):
            at[axis] = (turn[axis] + sign * digit) % 4
        z, y, x = at
        order.append(((4 * z + y) * 2 + x % 2, x // 2))
    return order


CHIPS_IN = chip_order((3, 3, 3), -1, (1, 0, 2))
CHIPS_OUT = chip_order((2, 2, 2), 1)
RANK = np.zeros((32, 2), np.int64)
for rank, chip in enumerate(CHIPS_IN):
    RANK[chip] = rank
PART_MAJOR = one_hot(4 * RANK.T[None] + np.arange(4)[:, None, None], 256)
PART_SUM = (PART_MAJOR.reshape(4, 2, 32, 256)[:, 0] + PART_MAJOR.reshape(4, 2, 32, 256)[:, 1]).reshape(128, 256)
SPREAD = one_hot([[32 * o + shot for o in range(4)] for shot, _ in CHIPS_OUT], 128)
RETURNED = np.concatenate([4 * RANK[chip] + np.arange(4) for chip in CHIPS_OUT])


def exchange(x, chips):
    groups = [[(2 * shot + high) * 2 + core for shot, high in chips] for core in range(2)]
    return lax.all_to_all(x, ("shot", "xh", "core"), 0, 0, axis_index_groups=groups, tiled=True)


WIDE = NT // 4


def held(x):
    return pltpu.with_memory_space_constraint(x, pltpu.HBM)


def bin_sign():
    return (2 * (lax.broadcasted_iota(jnp.int32, (1, 256), 1) & 1) - 1).astype(F32).astype(BF16)


def record_spectra(rec, waves):
    total = None
    for k in range(4):
        wave = waves[WIDE * (k % 2) : WIDE * (k % 2) + WIDE]
        wave = wave if k < 2 else wave * bin_sign()
        part = jnp.dot(rec[:, :, WIDE * k : WIDE * k + WIDE].reshape(512, WIDE), wave, preferred_element_type=F32)
        total = part if total is None else total + part
    return total.T.astype(BF16)


def give_kernel(
    records_ref, table_ref, flipped_ref, aperture_ref, give_ref, picks_ref, rec, keep, piece_ref, tab, ape, sems
):
    core = lax.axis_index("core")
    small = pltpu.make_async_copy(aperture_ref, ape, sems.at[5])
    small.start()
    first = [pltpu.make_async_copy(table_ref.at[1 - core], tab, sems.at[0])]
    for c in range(2):
        first.append(pltpu.make_async_copy(records_ref.at[0, c], rec.at[c], sems.at[1 + c]))
    later = [
        pltpu.make_async_copy(table_ref.at[core], keep, sems.at[3]),
        pltpu.make_async_copy(flipped_ref.at[pl.ds(pl.multiple_of(core * 256, 256), 256)], piece_ref, sems.at[4]),
    ]
    for copy in first + later:
        copy.start()
    c = lax.broadcasted_iota(jnp.int32, (64, 64), 0)
    j = lax.broadcasted_iota(jnp.int32, (64, 64), 1)
    order = (c == 2 * (j & 31) + (j >> 5)).astype(F32).astype(BF16)
    small.wait()
    picks = jnp.dot(ape[...].reshape(4, 64).astype(F32).astype(BF16), order, preferred_element_type=F32).astype(BF16)
    picks_ref[...] = picks
    give_ref[256:272, :] = jnp.zeros((16, 512), BF16)
    give_ref[256:260, 0:64] = picks
    for copy in first:
        copy.wait()
    give_ref[0:256, :] = record_spectra(rec, tab)
    for copy in later:
        copy.wait()


def transform_given(records, table, flipped, aperture):
    return pl.pallas_call(
        give_kernel,
        out_shape=(
            jax.ShapeDtypeStruct((272, 512), BF16),
            jax.ShapeDtypeStruct((4, 64), BF16),
            jax.ShapeDtypeStruct((2, 256, NT), BF16),
            jax.ShapeDtypeStruct((NT // 2, 256), BF16),
            jax.ShapeDtypeStruct((256, 1024), BF16),
        ),
        in_specs=[ANY, ANY, ANY, ANY],
        out_specs=(VMEM, VMEM, VMEM, VMEM, VMEM),
        scratch_shapes=[
            pltpu.VMEM((NT // 2, 256), BF16),
            pltpu.VMEM((4, 1, 64), jnp.int32),
            pltpu.SemaphoreType.DMA((6,)),
        ],
        compiler_params=PARAMS,
        cost_estimate=pl.CostEstimate(flops=2**29, bytes_accessed=5 * 2**20, transcendentals=0),
        name="give",
    )(held(records), held(table), held(flipped), held(aperture))


def keep_kernel(rec_ref, keep_ref, own_ref, other_ref, piece_ref, order_ref, out_ref, flat):
    core = lax.axis_index("core")
    out_ref[:, :, 0:512] = record_spectra(rec_ref, keep_ref).reshape(64, 4, 512)
    total = None
    for i, raw_ref in enumerate((own_ref, other_ref)):
        for t in range(8):
            rows = jnp.dot(
                order_ref[...], raw_ref[64 * t : 64 * t + 64].reshape(256, 256), preferred_element_type=F32
            ).astype(BF16)
            for s in range(4):
                flat[i, 64 * t : 64 * t + 64, 256 * s : 256 * s + 256] = rows[64 * s : 64 * s + 64]
        at = core if i == 0 else 1 - core
        waves = piece_ref[:, pl.ds(pl.multiple_of(at * 512, 512), 512)]
        part = jnp.dot(waves, flat[i], preferred_element_type=F32)
        total = part if total is None else total + part
    odd = 1 - (lax.broadcasted_iota(jnp.int32, (256, 1), 0) & 1)
    total = total * (1 - 2 * odd * lax.axis_index("xh")).astype(F32)
    out_ref[:, :, 1024:2048] = total.astype(BF16).reshape(64, 4, 1024)


def transform_kept(rec, keep, own, other, piece):
    return pl.pallas_call(
        keep_kernel,
        out_shape=jax.ShapeDtypeStruct((64, 4, 2176), BF16),
        in_specs=[VMEM] * 6,
        out_specs=VMEM,
        scratch_shapes=[pltpu.VMEM((2, 512, 1024), BF16)],
        compiler_params=PARAMS,
        cost_estimate=pl.CostEstimate(flops=3 * 2**29, bytes_accessed=4 * 2**20, transcendentals=0),
        name="keep",
    )(rec, keep, own, other, piece, SHOT_MAJOR)


def fill_kernel(message_ref, taken_ref, picks_ref, out_ref, block, picks, sems):
    block[...] = taken_ref[0:256, :].reshape(64, 4, 512)
    both = jnp.concatenate([picks_ref[...], taken_ref[256:260, 0:64]], axis=1)
    picks[...] = jnp.broadcast_to(both[None], (64, 4, 128))
    first = pltpu.make_async_copy(block, out_ref.at[:, :, 512:1024], sems.at[0])
    second = pltpu.make_async_copy(picks, out_ref.at[:, :, 2048:2176], sems.at[1])
    first.start()
    second.start()
    first.wait()
    second.wait()


def fill(message, taken, picks):
    return pl.pallas_call(
        fill_kernel,
        out_shape=jax.ShapeDtypeStruct((64, 4, 2176), BF16),
        in_specs=[ANY, VMEM, VMEM],
        out_specs=ANY,
        scratch_shapes=[
            pltpu.VMEM((64, 4, 512), BF16),
            pltpu.VMEM((64, 4, 128), BF16),
            pltpu.SemaphoreType.DMA((2,)),
        ],
        input_output_aliases={0: 0},
        compiler_params=PARAMS,
        name="fill",
    )(message, taken, picks)


def lane_pick(low, high, index):
    inside = index & 127
    a = jnp.take_along_axis(low, inside, axis=1, mode="promise_in_bounds")
    b = jnp.take_along_axis(high, inside, axis=1, mode="promise_in_bounds")
    return jnp.where(index < 128, a, b)


def mix_kernel(got_ref, order_ref, both_ref, spread_ref, out_ref):
    order = order_ref[...]
    rows = jnp.dot(order, got_ref[:, :, 0:1024].reshape(256, 1024), preferred_element_type=F32).astype(BF16)
    shots = jnp.dot(both_ref[...], got_ref[:, :, 1024:2048].reshape(256, 1024), preferred_element_type=F32)
    where = jnp.dot(order, got_ref[:, :, 2048:2176].reshape(256, 128), preferred_element_type=F32).astype(jnp.int32)
    picks, gathers = [], []
    for p in range(4):
        parts = []
        for s in range(4):
            low = shots[32 * p : 32 * p + 32, 256 * s : 256 * s + 128]
            high = shots[32 * p : 32 * p + 32, 256 * s + 128 : 256 * s + 256]
            parts.append(
                jnp.concatenate(
                    [lane_pick(low, high, where[64 * s + 32 * h : 64 * s + 32 * h + 32]) for h in range(2)], axis=1
                )
            )
        picks.append(jnp.concatenate(parts, axis=0))
        gathers.append(
            jnp.concatenate(
                [
                    rows[64 * p + 32 * h : 64 * p + 32 * h + 32, 256 * b : 256 * b + 256]
                    for h in range(2)
                    for b in range(4)
                ],
                axis=0,
            )
        )
    total = [None] * 4
    for f in range(2):
        re, im, minus = picks[f].astype(BF16), picks[2 + f].astype(BF16), (-picks[2 + f]).astype(BF16)
        left = jnp.concatenate(
            [jnp.concatenate([re, minus], axis=1), jnp.concatenate([im, re], axis=1)], axis=0
        )
        right = jnp.concatenate([gathers[f], gathers[2 + f]], axis=0)
        out = jnp.dot(left, right, preferred_element_type=F32).astype(BF16)
        for part in range(2):
            total[2 * part + f] = jnp.concatenate(
                [out[128 * part + 32 * s : 128 * part + 32 * s + 32] for s in range(4)], axis=1
            )
    total = jnp.concatenate(total, axis=0)
    out_ref[...] = (
        jnp.dot(spread_ref[...], total, preferred_element_type=F32).astype(BF16).reshape(64, 4, 1024)
    )


def mix(got):
    return pl.pallas_call(
        mix_kernel,
        out_shape=jax.ShapeDtypeStruct((64, 4, 1024), BF16),
        in_specs=[VMEM, VMEM, VMEM, VMEM],
        out_specs=VMEM,
        compiler_params=PARAMS,
        name="mix",
    )(got, PART_MAJOR, PART_SUM, SPREAD)


def inverse_waves(table_ref, half, rows, count):
    block = 2 * lax.axis_index("xh") + lax.axis_index("core")
    return table_ref[
        pl.ds(pl.multiple_of(block * 512 + rows, 256), count), pl.ds(pl.multiple_of(half * 256, 256), 256)
    ]


def own_half_kernel(own_ref, table_ref, out_ref):
    waves = inverse_waves(table_ref, lax.axis_index("core"), 0, 512)
    out_ref[...] = jnp.dot(waves, own_ref[...].reshape(256, 1024), preferred_element_type=F32)


def own_half(own, table):
    return pl.pallas_call(
        own_half_kernel,
        out_shape=jax.ShapeDtypeStruct((512, 1024), F32),
        in_specs=[VMEM, VMEM],
        out_specs=VMEM,
        compiler_params=PARAMS,
        cost_estimate=pl.CostEstimate(flops=2**28, bytes_accessed=2**20, transcendentals=0),
        name="own_half",
    )(own, table)


def inverse_kernel(part_ref, other_ref, table_ref, order_ref, out_ref, ready, sems):
    other = other_ref[...].reshape(256, 1024)
    outs = []
    for half in range(2):
        waves = inverse_waves(table_ref, 1 - lax.axis_index("core"), 256 * half, 256)
        here = jnp.dot(waves, other, preferred_element_type=F32)
        here = (here + part_ref[256 * half : 256 * half + 256]).astype(BF16)
        for t in range(4):
            at = 256 * half + 64 * t
            stack = jnp.concatenate(
                [here[64 * t : 64 * t + 64, 256 * s : 256 * s + 256] for s in range(4)], axis=0
            )
            ready[at : at + 64] = (
                jnp.dot(order_ref[...], stack, preferred_element_type=F32).astype(BF16).reshape(64, 4, 256)
            )
            if t >= 0:
                rows = pl.ds(at, 64)
                outs.append(pltpu.make_async_copy(ready.at[rows], out_ref.at[rows], sems.at[len(outs)]))
                outs[-1].start()
    for copy in outs:
        copy.wait()


def transform_back(part, other, table):
    return pl.pallas_call(
        inverse_kernel,
        out_shape=jax.ShapeDtypeStruct((512, 4, 256), BF16),
        in_specs=[VMEM, VMEM, VMEM, VMEM],
        out_specs=ANY,
        scratch_shapes=[pltpu.VMEM((512, 4, 256), BF16), pltpu.SemaphoreType.DMA((8,))],
        compiler_params=PARAMS,
        name="inverse",
    )(part, other, table, TIME_MAJOR)


def on_device(records, targets, aperture):
    forward, flipped, inverse = tables()
    swap = [(0, 1), (1, 0)]
    others = lax.ppermute(targets, "core", swap)
    give, picks, rec, keep, piece = transform_given(records, forward, flipped, aperture)
    taken = lax.ppermute(give, "core", swap)
    message = transform_kept(rec, keep, targets, others, piece)
    message = fill(message, taken, picks)
    back = exchange(mix(exchange(message, CHIPS_IN)), CHIPS_OUT)
    other = lax.ppermute(back, "core", swap)
    return transform_back(own_half(back, inverse), other, inverse)


def solution(mesh):
    cut = Mesh(mesh.devices.reshape(32, 2, 2), ("shot", "xh", "core"))
    xline = ("xh", "core")
    return jax.shard_map(
        on_device,
        mesh=cut,
        in_specs=(P(xline, "shot", None, None), P(xline, "shot", None), P("shot", xline, None)),
        out_specs=P(xline, "shot", None),
        check_vma=False,
    )
```

```python
import jax
import jax.numpy as jnp
import ml_dtypes
import numpy as np
from jax import lax
from jax.experimental import pallas as pl
from jax.experimental.pallas import tpu as pltpu
from jax.sharding import Mesh, PartitionSpec as P

NT = 2048
NF = 256
BF16 = jnp.bfloat16
F32 = jnp.float32
VMEM = pl.BlockSpec(memory_space=pltpu.VMEM)
ANY = pl.BlockSpec(memory_space=pl.ANY)
PARAMS = pltpu.CompilerParams(vmem_limit_bytes=24 * 2**20)


def part_order():
    freq = np.arange(NF).reshape(2, 64, 1, 2)
    return np.concatenate([freq, freq + NF], axis=2).reshape(2 * NF)


def tables():
    angle = (np.arange(NT)[:, None] * np.arange(1, NF + 1)[None, :] % NT) * (2.0 * np.pi / NT)
    waves = np.concatenate([np.cos(angle), -np.sin(angle)], axis=1)[:, part_order()]
    forward = (waves / np.sqrt(NT)).astype(np.float32).astype(ml_dtypes.bfloat16)
    returned = np.concatenate([RETURNED, 256 + RETURNED])
    inverse = (waves[:, returned] * (2.0 / np.sqrt(NT))).astype(np.float32).astype(ml_dtypes.bfloat16)
    first = forward[: NT // 2]
    return np.ascontiguousarray(first.reshape(NT // 2, 2, 256).transpose(1, 0, 2)), np.ascontiguousarray(first.T), inverse


def one_hot(rows, depth):
    return np.eye(depth, dtype=np.float32)[np.asarray(rows).reshape(-1)].astype(ml_dtypes.bfloat16)


SHOT_MAJOR = one_hot(np.arange(256).reshape(64, 4).T, 256)
TIME_MAJOR = one_hot(np.arange(256).reshape(4, 64).T, 256)
def chip_order(turn, sign, axes=(0, 1, 2), stride=1):
    order = []
    for a in range(64):
        a = a * stride % 64
        at = [0, 0, 0]
        for axis, digit in zip(axes, (a // 16, a // 4 % 4, a % 4)):
            at[axis] = (turn[axis] + sign * digit) % 4
        z, y, x = at
        order.append(((4 * z + y) * 2 + x % 2, x // 2))
    return order


CHIPS_IN = chip_order((3, 2, 3), -1, (0, 1, 2), 21)
CHIPS_OUT = chip_order((2, 2, 2), 1)
RANK = np.zeros((32, 2), np.int64)
for rank, chip in enumerate(CHIPS_IN):
    RANK[chip] = rank
PART_MAJOR = one_hot(4 * RANK.T[None] + np.arange(4)[:, None, None], 256)
PART_SUM = (PART_MAJOR.reshape(4, 2, 32, 256)[:, 0] + PART_MAJOR.reshape(4, 2, 32, 256)[:, 1]).reshape(128, 256)
SPREAD = one_hot([[32 * o + shot for o in range(4)] for shot, _ in CHIPS_OUT], 128)
RETURNED = np.concatenate([4 * RANK[chip] + np.arange(4) for chip in CHIPS_OUT])


def exchange(x, chips):
    groups = [[(2 * shot + high) * 2 + core for shot, high in chips] for core in range(2)]
    return lax.all_to_all(x, ("shot", "xh", "core"), 0, 0, axis_index_groups=groups, tiled=True)


WIDE = NT // 4


def held(x):
    return pltpu.with_memory_space_constraint(x, pltpu.HBM)


def bin_sign():
    return (2 * (lax.broadcasted_iota(jnp.int32, (1, 256), 1) & 1) - 1).astype(F32).astype(BF16)


def record_spectra(rec, waves):
    total = None
    for k in range(4):
        wave = waves[WIDE * (k % 2) : WIDE * (k % 2) + WIDE]
        wave = wave if k < 2 else wave * bin_sign()
        part = jnp.dot(rec[:, :, WIDE * k : WIDE * k + WIDE].reshape(512, WIDE), wave, preferred_element_type=F32)
        total = part if total is None else total + part
    return total.T.astype(BF16)


def give_kernel(
    records_ref, table_ref, flipped_ref, aperture_ref, give_ref, picks_ref, rec, keep, piece_ref, tab, ape, sems
):
    core = lax.axis_index("core")
    small = pltpu.make_async_copy(aperture_ref, ape, sems.at[5])
    small.start()
    first = [pltpu.make_async_copy(table_ref.at[1 - core], tab, sems.at[0])]
    for c in range(2):
        first.append(pltpu.make_async_copy(records_ref.at[0, c], rec.at[c], sems.at[1 + c]))
    later = [
        pltpu.make_async_copy(table_ref.at[core], keep, sems.at[3]),
        pltpu.make_async_copy(flipped_ref.at[pl.ds(pl.multiple_of(core * 256, 256), 256)], piece_ref, sems.at[4]),
    ]
    for copy in first + later:
        copy.start()
    c = lax.broadcasted_iota(jnp.int32, (64, 64), 0)
    j = lax.broadcasted_iota(jnp.int32, (64, 64), 1)
    order = (c == 2 * (j & 31) + (j >> 5)).astype(F32).astype(BF16)
    small.wait()
    picks = jnp.dot(ape[...].reshape(4, 64).astype(F32).astype(BF16), order, preferred_element_type=F32).astype(BF16)
    picks_ref[...] = picks
    give_ref[256:272, :] = jnp.zeros((16, 512), BF16)
    give_ref[256:260, 0:64] = picks
    for copy in first:
        copy.wait()
    give_ref[0:256, :] = record_spectra(rec, tab)
    for copy in later:
        copy.wait()


def transform_given(records, table, flipped, aperture):
    return pl.pallas_call(
        give_kernel,
        out_shape=(
            jax.ShapeDtypeStruct((272, 512), BF16),
            jax.ShapeDtypeStruct((4, 64), BF16),
            jax.ShapeDtypeStruct((2, 256, NT), BF16),
            jax.ShapeDtypeStruct((NT // 2, 256), BF16),
            jax.ShapeDtypeStruct((256, 1024), BF16),
        ),
        in_specs=[ANY, ANY, ANY, ANY],
        out_specs=(VMEM, VMEM, VMEM, VMEM, VMEM),
        scratch_shapes=[
            pltpu.VMEM((NT // 2, 256), BF16),
            pltpu.VMEM((4, 1, 64), jnp.int32),
            pltpu.SemaphoreType.DMA((6,)),
        ],
        compiler_params=PARAMS,
        cost_estimate=pl.CostEstimate(flops=2**29, bytes_accessed=5 * 2**20, transcendentals=0),
        name="give",
    )(held(records), held(table), held(flipped), held(aperture))


def keep_kernel(rec_ref, keep_ref, own_ref, other_ref, piece_ref, order_ref, out_ref, flat):
    core = lax.axis_index("core")
    out_ref[:, :, 0:512] = record_spectra(rec_ref, keep_ref).reshape(64, 4, 512)
    total = None
    for i, raw_ref in enumerate((own_ref, other_ref)):
        for t in range(8):
            rows = jnp.dot(
                order_ref[...], raw_ref[64 * t : 64 * t + 64].reshape(256, 256), preferred_element_type=F32
            ).astype(BF16)
            for s in range(4):
                flat[i, 64 * t : 64 * t + 64, 256 * s : 256 * s + 256] = rows[64 * s : 64 * s + 64]
        at = core if i == 0 else 1 - core
        waves = piece_ref[:, pl.ds(pl.multiple_of(at * 512, 512), 512)]
        part = jnp.dot(waves, flat[i], preferred_element_type=F32)
        total = part if total is None else total + part
    odd = 1 - (lax.broadcasted_iota(jnp.int32, (256, 1), 0) & 1)
    total = total * (1 - 2 * odd * lax.axis_index("xh")).astype(F32)
    out_ref[:, :, 1024:2048] = total.astype(BF16).reshape(64, 4, 1024)


def transform_kept(rec, keep, own, other, piece):
    return pl.pallas_call(
        keep_kernel,
        out_shape=jax.ShapeDtypeStruct((64, 4, 2176), BF16),
        in_specs=[VMEM] * 6,
        out_specs=VMEM,
        scratch_shapes=[pltpu.VMEM((2, 512, 1024), BF16)],
        compiler_params=PARAMS,
        cost_estimate=pl.CostEstimate(flops=3 * 2**29, bytes_accessed=4 * 2**20, transcendentals=0),
        name="keep",
    )(rec, keep, own, other, piece, SHOT_MAJOR)


def fill_kernel(message_ref, taken_ref, picks_ref, out_ref, block, picks, sems):
    block[...] = taken_ref[0:256, :].reshape(64, 4, 512)
    both = jnp.concatenate([picks_ref[...], taken_ref[256:260, 0:64]], axis=1)
    picks[...] = jnp.broadcast_to(both[None], (64, 4, 128))
    first = pltpu.make_async_copy(block, out_ref.at[:, :, 512:1024], sems.at[0])
    second = pltpu.make_async_copy(picks, out_ref.at[:, :, 2048:2176], sems.at[1])
    first.start()
    second.start()
    first.wait()
    second.wait()


def fill(message, taken, picks):
    return pl.pallas_call(
        fill_kernel,
        out_shape=jax.ShapeDtypeStruct((64, 4, 2176), BF16),
        in_specs=[ANY, VMEM, VMEM],
        out_specs=ANY,
        scratch_shapes=[
            pltpu.VMEM((64, 4, 512), BF16),
            pltpu.VMEM((64, 4, 128), BF16),
            pltpu.SemaphoreType.DMA((2,)),
        ],
        input_output_aliases={0: 0},
        compiler_params=PARAMS,
        name="fill",
    )(message, taken, picks)


def lane_pick(low, high, index):
    inside = index & 127
    a = jnp.take_along_axis(low, inside, axis=1, mode="promise_in_bounds")
    b = jnp.take_along_axis(high, inside, axis=1, mode="promise_in_bounds")
    return jnp.where(index < 128, a, b)


def mix_kernel(got_ref, order_ref, both_ref, spread_ref, out_ref):
    order = order_ref[...]
    rows = jnp.dot(order, got_ref[:, :, 0:1024].reshape(256, 1024), preferred_element_type=F32).astype(BF16)
    shots = jnp.dot(both_ref[...], got_ref[:, :, 1024:2048].reshape(256, 1024), preferred_element_type=F32)
    where = jnp.dot(order, got_ref[:, :, 2048:2176].reshape(256, 128), preferred_element_type=F32).astype(jnp.int32)
    picks, gathers = [], []
    for p in range(4):
        parts = []
        for s in range(4):
            low = shots[32 * p : 32 * p + 32, 256 * s : 256 * s + 128]
            high = shots[32 * p : 32 * p + 32, 256 * s + 128 : 256 * s + 256]
            parts.append(
                jnp.concatenate(
                    [lane_pick(low, high, where[64 * s + 32 * h : 64 * s + 32 * h + 32]) for h in range(2)], axis=1
                )
            )
        picks.append(jnp.concatenate(parts, axis=0))
        gathers.append(
            jnp.concatenate(
                [
                    rows[64 * p + 32 * h : 64 * p + 32 * h + 32, 256 * b : 256 * b + 256]
                    for h in range(2)
                    for b in range(4)
                ],
                axis=0,
            )
        )
    total = [None] * 4
    for f in range(2):
        re, im, minus = picks[f].astype(BF16), picks[2 + f].astype(BF16), (-picks[2 + f]).astype(BF16)
        left = jnp.concatenate(
            [jnp.concatenate([re, minus], axis=1), jnp.concatenate([im, re], axis=1)], axis=0
        )
        right = jnp.concatenate([gathers[f], gathers[2 + f]], axis=0)
        out = jnp.dot(left, right, preferred_element_type=F32).astype(BF16)
        for part in range(2):
            total[2 * part + f] = jnp.concatenate(
                [out[128 * part + 32 * s : 128 * part + 32 * s + 32] for s in range(4)], axis=1
            )
    total = jnp.concatenate(total, axis=0)
    out_ref[...] = (
        jnp.dot(spread_ref[...], total, preferred_element_type=F32).astype(BF16).reshape(64, 4, 1024)
    )


def mix(got):
    return pl.pallas_call(
        mix_kernel,
        out_shape=jax.ShapeDtypeStruct((64, 4, 1024), BF16),
        in_specs=[VMEM, VMEM, VMEM, VMEM],
        out_specs=VMEM,
        compiler_params=PARAMS,
        name="mix",
    )(got, PART_MAJOR, PART_SUM, SPREAD)


def inverse_waves(table_ref, half, rows, count):
    block = 2 * lax.axis_index("xh") + lax.axis_index("core")
    return table_ref[
        pl.ds(pl.multiple_of(block * 512 + rows, 256), count), pl.ds(pl.multiple_of(half * 256, 256), 256)
    ]


def own_half_kernel(own_ref, table_ref, out_ref):
    waves = inverse_waves(table_ref, lax.axis_index("core"), 0, 512)
    out_ref[...] = jnp.dot(waves, own_ref[...].reshape(256, 1024), preferred_element_type=F32)


def own_half(own, table):
    return pl.pallas_call(
        own_half_kernel,
        out_shape=jax.ShapeDtypeStruct((512, 1024), F32),
        in_specs=[VMEM, VMEM],
        out_specs=VMEM,
        compiler_params=PARAMS,
        cost_estimate=pl.CostEstimate(flops=2**28, bytes_accessed=2**20, transcendentals=0),
        name="own_half",
    )(own, table)


def inverse_kernel(part_ref, other_ref, table_ref, order_ref, out_ref, ready, sems):
    other = other_ref[...].reshape(256, 1024)
    outs = []
    for half in range(2):
        waves = inverse_waves(table_ref, 1 - lax.axis_index("core"), 256 * half, 256)
        here = jnp.dot(waves, other, preferred_element_type=F32)
        here = (here + part_ref[256 * half : 256 * half + 256]).astype(BF16)
        for t in range(4):
            at = 256 * half + 64 * t
            stack = jnp.concatenate(
                [here[64 * t : 64 * t + 64, 256 * s : 256 * s + 256] for s in range(4)], axis=0
            )
            ready[at : at + 64] = (
                jnp.dot(order_ref[...], stack, preferred_element_type=F32).astype(BF16).reshape(64, 4, 256)
            )
            if t >= 0:
                rows = pl.ds(at, 64)
                outs.append(pltpu.make_async_copy(ready.at[rows], out_ref.at[rows], sems.at[len(outs)]))
                outs[-1].start()
    for copy in outs:
        copy.wait()


def transform_back(part, other, table):
    return pl.pallas_call(
        inverse_kernel,
        out_shape=jax.ShapeDtypeStruct((512, 4, 256), BF16),
        in_specs=[VMEM, VMEM, VMEM, VMEM],
        out_specs=ANY,
        scratch_shapes=[pltpu.VMEM((512, 4, 256), BF16), pltpu.SemaphoreType.DMA((8,))],
        compiler_params=PARAMS,
        name="inverse",
    )(part, other, table, TIME_MAJOR)


def on_device(records, targets, aperture):
    forward, flipped, inverse = tables()
    swap = [(0, 1), (1, 0)]
    others = lax.ppermute(targets, "core", swap)
    give, picks, rec, keep, piece = transform_given(records, forward, flipped, aperture)
    taken = lax.ppermute(give, "core", swap)
    message = transform_kept(rec, keep, targets, others, piece)
    message = fill(message, taken, picks)
    back = exchange(mix(exchange(message, CHIPS_IN)), CHIPS_OUT)
    other = lax.ppermute(back, "core", swap)
    return transform_back(own_half(back, inverse), other, inverse)


def solution(mesh):
    cut = Mesh(mesh.devices.reshape(32, 2, 2), ("shot", "xh", "core"))
    xline = ("xh", "core")
    return jax.shard_map(
        on_device,
        mesh=cut,
        in_specs=(P(xline, "shot", None, None), P(xline, "shot", None), P("shot", xline, None)),
        out_specs=P(xline, "shot", None),
        check_vma=False,
    )
```

```python
import jax
import jax.numpy as jnp
import ml_dtypes
import numpy as np
from jax import lax
from jax.experimental import pallas as pl
from jax.experimental.pallas import tpu as pltpu
from jax.sharding import Mesh, PartitionSpec as P

NT = 2048
NF = 256
BF16 = jnp.bfloat16
F32 = jnp.float32
VMEM = pl.BlockSpec(memory_space=pltpu.VMEM)
ANY = pl.BlockSpec(memory_space=pl.ANY)
PARAMS = pltpu.CompilerParams(vmem_limit_bytes=24 * 2**20)


def part_order():
    freq = np.arange(NF).reshape(2, 64, 1, 2)
    return np.concatenate([freq, freq + NF], axis=2).reshape(2 * NF)


def tables():
    angle = (np.arange(NT)[:, None] * np.arange(1, NF + 1)[None, :] % NT) * (2.0 * np.pi / NT)
    waves = np.concatenate([np.cos(angle), -np.sin(angle)], axis=1)[:, part_order()]
    forward = (waves / np.sqrt(NT)).astype(np.float32).astype(ml_dtypes.bfloat16)
    returned = np.concatenate([RETURNED, 256 + RETURNED])
    inverse = (waves[:, returned] * (2.0 / np.sqrt(NT))).astype(np.float32).astype(ml_dtypes.bfloat16)
    first = forward[: NT // 2]
    return np.ascontiguousarray(first.reshape(NT // 2, 2, 256).transpose(1, 0, 2)), np.ascontiguousarray(first.T), inverse


def one_hot(rows, depth):
    return np.eye(depth, dtype=np.float32)[np.asarray(rows).reshape(-1)].astype(ml_dtypes.bfloat16)


SHOT_MAJOR = one_hot(np.arange(256).reshape(64, 4).T, 256)
TIME_MAJOR = one_hot(np.arange(256).reshape(4, 64).T, 256)
def chip_order(turn, sign, axes=(0, 1, 2), stride=1):
    order = []
    for a in range(64):
        a = a * stride % 64
        at = [0, 0, 0]
        for axis, digit in zip(axes, (a // 16, a // 4 % 4, a % 4)):
            at[axis] = (turn[axis] + sign * digit) % 4
        z, y, x = at
        order.append(((4 * z + y) * 2 + x % 2, x // 2))
    return order


CHIPS_IN = chip_order((3, 2, 3), 1, (0, 1, 2), 21)
CHIPS_OUT = chip_order((2, 2, 2), 1, (2, 0, 1))
RANK = np.zeros((32, 2), np.int64)
for rank, chip in enumerate(CHIPS_IN):
    RANK[chip] = rank
PART_MAJOR = one_hot(4 * RANK.T[None] + np.arange(4)[:, None, None], 256)
PART_SUM = (PART_MAJOR.reshape(4, 2, 32, 256)[:, 0] + PART_MAJOR.reshape(4, 2, 32, 256)[:, 1]).reshape(128, 256)
SPREAD = one_hot([[32 * o + shot for o in range(4)] for shot, _ in CHIPS_OUT], 128)
RETURNED = np.concatenate([4 * RANK[chip] + np.arange(4) for chip in CHIPS_OUT])


def exchange(x, chips):
    groups = [[(2 * shot + high) * 2 + core for shot, high in chips] for core in range(2)]
    return lax.all_to_all(x, ("shot", "xh", "core"), 0, 0, axis_index_groups=groups, tiled=True)


WIDE = NT // 4


def held(x):
    return pltpu.with_memory_space_constraint(x, pltpu.HBM)


def bin_sign():
    return (2 * (lax.broadcasted_iota(jnp.int32, (1, 256), 1) & 1) - 1).astype(F32).astype(BF16)


def record_spectra(rec, waves):
    total = None
    for k in range(4):
        wave = waves[WIDE * (k % 2) : WIDE * (k % 2) + WIDE]
        wave = wave if k < 2 else wave * bin_sign()
        part = jnp.dot(rec[:, :, WIDE * k : WIDE * k + WIDE].reshape(512, WIDE), wave, preferred_element_type=F32)
        total = part if total is None else total + part
    return total.T.astype(BF16)


def give_kernel(
    records_ref, table_ref, flipped_ref, aperture_ref, give_ref, picks_ref, rec, keep, piece_ref, tab, ape, sems
):
    core = lax.axis_index("core")
    small = pltpu.make_async_copy(aperture_ref, ape, sems.at[5])
    small.start()
    first = [pltpu.make_async_copy(table_ref.at[1 - core], tab, sems.at[0])]
    for c in range(2):
        first.append(pltpu.make_async_copy(records_ref.at[0, c], rec.at[c], sems.at[1 + c]))
    later = [
        pltpu.make_async_copy(table_ref.at[core], keep, sems.at[3]),
        pltpu.make_async_copy(flipped_ref.at[pl.ds(pl.multiple_of(core * 256, 256), 256)], piece_ref, sems.at[4]),
    ]
    for copy in first + later:
        copy.start()
    c = lax.broadcasted_iota(jnp.int32, (64, 64), 0)
    j = lax.broadcasted_iota(jnp.int32, (64, 64), 1)
    order = (c == 2 * (j & 31) + (j >> 5)).astype(F32).astype(BF16)
    small.wait()
    picks = jnp.dot(ape[...].reshape(4, 64).astype(F32).astype(BF16), order, preferred_element_type=F32).astype(BF16)
    picks_ref[...] = picks
    give_ref[256:272, :] = jnp.zeros((16, 512), BF16)
    give_ref[256:260, 0:64] = picks
    for copy in first:
        copy.wait()
    give_ref[0:256, :] = record_spectra(rec, tab)
    for copy in later:
        copy.wait()


def transform_given(records, table, flipped, aperture):
    return pl.pallas_call(
        give_kernel,
        out_shape=(
            jax.ShapeDtypeStruct((272, 512), BF16),
            jax.ShapeDtypeStruct((4, 64), BF16),
            jax.ShapeDtypeStruct((2, 256, NT), BF16),
            jax.ShapeDtypeStruct((NT // 2, 256), BF16),
            jax.ShapeDtypeStruct((256, 1024), BF16),
        ),
        in_specs=[ANY, ANY, ANY, ANY],
        out_specs=(VMEM, VMEM, VMEM, VMEM, VMEM),
        scratch_shapes=[
            pltpu.VMEM((NT // 2, 256), BF16),
            pltpu.VMEM((4, 1, 64), jnp.int32),
            pltpu.SemaphoreType.DMA((6,)),
        ],
        compiler_params=PARAMS,
        cost_estimate=pl.CostEstimate(flops=2**29, bytes_accessed=5 * 2**20, transcendentals=0),
        name="give",
    )(held(records), held(table), held(flipped), held(aperture))


def keep_kernel(rec_ref, keep_ref, own_ref, other_ref, piece_ref, order_ref, out_ref, flat):
    core = lax.axis_index("core")
    out_ref[:, :, 0:512] = record_spectra(rec_ref, keep_ref).reshape(64, 4, 512)
    total = None
    for i, raw_ref in enumerate((own_ref, other_ref)):
        for t in range(8):
            rows = jnp.dot(
                order_ref[...], raw_ref[64 * t : 64 * t + 64].reshape(256, 256), preferred_element_type=F32
            ).astype(BF16)
            for s in range(4):
                flat[i, 64 * t : 64 * t + 64, 256 * s : 256 * s + 256] = rows[64 * s : 64 * s + 64]
        at = core if i == 0 else 1 - core
        waves = piece_ref[:, pl.ds(pl.multiple_of(at * 512, 512), 512)]
        part = jnp.dot(waves, flat[i], preferred_element_type=F32)
        total = part if total is None else total + part
    odd = 1 - (lax.broadcasted_iota(jnp.int32, (256, 1), 0) & 1)
    total = total * (1 - 2 * odd * lax.axis_index("xh")).astype(F32)
    out_ref[:, :, 1024:2048] = total.astype(BF16).reshape(64, 4, 1024)


def transform_kept(rec, keep, own, other, piece):
    return pl.pallas_call(
        keep_kernel,
        out_shape=jax.ShapeDtypeStruct((64, 4, 2176), BF16),
        in_specs=[VMEM] * 6,
        out_specs=VMEM,
        scratch_shapes=[pltpu.VMEM((2, 512, 1024), BF16)],
        compiler_params=PARAMS,
        cost_estimate=pl.CostEstimate(flops=3 * 2**29, bytes_accessed=4 * 2**20, transcendentals=0),
        name="keep",
    )(rec, keep, own, other, piece, SHOT_MAJOR)


def fill_kernel(message_ref, taken_ref, picks_ref, out_ref, block, picks, sems):
    block[...] = taken_ref[0:256, :].reshape(64, 4, 512)
    both = jnp.concatenate([picks_ref[...], taken_ref[256:260, 0:64]], axis=1)
    picks[...] = jnp.broadcast_to(both[None], (64, 4, 128))
    first = pltpu.make_async_copy(block, out_ref.at[:, :, 512:1024], sems.at[0])
    second = pltpu.make_async_copy(picks, out_ref.at[:, :, 2048:2176], sems.at[1])
    first.start()
    second.start()
    first.wait()
    second.wait()


def fill(message, taken, picks):
    return pl.pallas_call(
        fill_kernel,
        out_shape=jax.ShapeDtypeStruct((64, 4, 2176), BF16),
        in_specs=[ANY, VMEM, VMEM],
        out_specs=ANY,
        scratch_shapes=[
            pltpu.VMEM((64, 4, 512), BF16),
            pltpu.VMEM((64, 4, 128), BF16),
            pltpu.SemaphoreType.DMA((2,)),
        ],
        input_output_aliases={0: 0},
        compiler_params=PARAMS,
        name="fill",
    )(message, taken, picks)


def lane_pick(low, high, index):
    inside = index & 127
    a = jnp.take_along_axis(low, inside, axis=1, mode="promise_in_bounds")
    b = jnp.take_along_axis(high, inside, axis=1, mode="promise_in_bounds")
    return jnp.where(index < 128, a, b)


def mix_kernel(got_ref, order_ref, both_ref, spread_ref, out_ref):
    order = order_ref[...]
    rows = jnp.dot(order, got_ref[:, :, 0:1024].reshape(256, 1024), preferred_element_type=F32).astype(BF16)
    shots = jnp.dot(both_ref[...], got_ref[:, :, 1024:2048].reshape(256, 1024), preferred_element_type=F32)
    where = jnp.dot(order, got_ref[:, :, 2048:2176].reshape(256, 128), preferred_element_type=F32).astype(jnp.int32)
    picks, gathers = [], []
    for p in range(4):
        parts = []
        for s in range(4):
            low = shots[32 * p : 32 * p + 32, 256 * s : 256 * s + 128]
            high = shots[32 * p : 32 * p + 32, 256 * s + 128 : 256 * s + 256]
            parts.append(
                jnp.concatenate(
                    [lane_pick(low, high, where[64 * s + 32 * h : 64 * s + 32 * h + 32]) for h in range(2)], axis=1
                )
            )
        picks.append(jnp.concatenate(parts, axis=0))
        gathers.append(
            jnp.concatenate(
                [
                    rows[64 * p + 32 * h : 64 * p + 32 * h + 32, 256 * b : 256 * b + 256]
                    for h in range(2)
                    for b in range(4)
                ],
                axis=0,
            )
        )
    total = [None] * 4
    for f in range(2):
        re, im, minus = picks[f].astype(BF16), picks[2 + f].astype(BF16), (-picks[2 + f]).astype(BF16)
        left = jnp.concatenate(
            [jnp.concatenate([re, minus], axis=1), jnp.concatenate([im, re], axis=1)], axis=0
        )
        right = jnp.concatenate([gathers[f], gathers[2 + f]], axis=0)
        out = jnp.dot(left, right, preferred_element_type=F32).astype(BF16)
        for part in range(2):
            total[2 * part + f] = jnp.concatenate(
                [out[128 * part + 32 * s : 128 * part + 32 * s + 32] for s in range(4)], axis=1
            )
    total = jnp.concatenate(total, axis=0)
    out_ref[...] = (
        jnp.dot(spread_ref[...], total, preferred_element_type=F32).astype(BF16).reshape(64, 4, 1024)
    )


def mix(got):
    return pl.pallas_call(
        mix_kernel,
        out_shape=jax.ShapeDtypeStruct((64, 4, 1024), BF16),
        in_specs=[VMEM, VMEM, VMEM, VMEM],
        out_specs=VMEM,
        compiler_params=PARAMS,
        name="mix",
    )(got, PART_MAJOR, PART_SUM, SPREAD)


def inverse_waves(table_ref, half, rows, count):
    block = 2 * lax.axis_index("xh") + lax.axis_index("core")
    return table_ref[
        pl.ds(pl.multiple_of(block * 512 + rows, 256), count), pl.ds(pl.multiple_of(half * 256, 256), 256)
    ]


def own_half_kernel(own_ref, table_ref, out_ref):
    waves = inverse_waves(table_ref, lax.axis_index("core"), 0, 512)
    out_ref[...] = jnp.dot(waves, own_ref[...].reshape(256, 1024), preferred_element_type=F32)


def own_half(own, table):
    return pl.pallas_call(
        own_half_kernel,
        out_shape=jax.ShapeDtypeStruct((512, 1024), F32),
        in_specs=[VMEM, VMEM],
        out_specs=VMEM,
        compiler_params=PARAMS,
        cost_estimate=pl.CostEstimate(flops=2**28, bytes_accessed=2**20, transcendentals=0),
        name="own_half",
    )(own, table)


def inverse_kernel(part_ref, other_ref, table_ref, order_ref, out_ref, ready, sems):
    other = other_ref[...].reshape(256, 1024)
    outs = []
    for half in range(2):
        waves = inverse_waves(table_ref, 1 - lax.axis_index("core"), 256 * half, 256)
        here = jnp.dot(waves, other, preferred_element_type=F32)
        here = (here + part_ref[256 * half : 256 * half + 256]).astype(BF16)
        for t in range(4):
            at = 256 * half + 64 * t
            stack = jnp.concatenate(
                [here[64 * t : 64 * t + 64, 256 * s : 256 * s + 256] for s in range(4)], axis=0
            )
            ready[at : at + 64] = (
                jnp.dot(order_ref[...], stack, preferred_element_type=F32).astype(BF16).reshape(64, 4, 256)
            )
            if t >= 0:
                rows = pl.ds(at, 64)
                outs.append(pltpu.make_async_copy(ready.at[rows], out_ref.at[rows], sems.at[len(outs)]))
                outs[-1].start()
    for copy in outs:
        copy.wait()


def transform_back(part, other, table):
    return pl.pallas_call(
        inverse_kernel,
        out_shape=jax.ShapeDtypeStruct((512, 4, 256), BF16),
        in_specs=[VMEM, VMEM, VMEM, VMEM],
        out_specs=ANY,
        scratch_shapes=[pltpu.VMEM((512, 4, 256), BF16), pltpu.SemaphoreType.DMA((8,))],
        compiler_params=PARAMS,
        name="inverse",
    )(part, other, table, TIME_MAJOR)


def on_device(records, targets, aperture):
    forward, flipped, inverse = tables()
    swap = [(0, 1), (1, 0)]
    others = lax.ppermute(targets, "core", swap)
    give, picks, rec, keep, piece = transform_given(records, forward, flipped, aperture)
    taken = lax.ppermute(give, "core", swap)
    message = transform_kept(rec, keep, targets, others, piece)
    message = fill(message, taken, picks)
    back = exchange(mix(exchange(message, CHIPS_IN)), CHIPS_OUT)
    other = lax.ppermute(back, "core", swap)
    return transform_back(own_half(back, inverse), other, inverse)


def solution(mesh):
    cut = Mesh(mesh.devices.reshape(32, 2, 2), ("shot", "xh", "core"))
    xline = ("xh", "core")
    return jax.shard_map(
        on_device,
        mesh=cut,
        in_specs=(P(xline, "shot", None, None), P(xline, "shot", None), P("shot", xline, None)),
        out_specs=P(xline, "shot", None),
        check_vma=False,
    )
```

```python
import jax
import jax.numpy as jnp
import ml_dtypes
import numpy as np
from jax import lax
from jax.experimental import pallas as pl
from jax.experimental.pallas import tpu as pltpu
from jax.sharding import Mesh, PartitionSpec as P

NT = 2048
NF = 256
BF16 = jnp.bfloat16
F32 = jnp.float32
VMEM = pl.BlockSpec(memory_space=pltpu.VMEM)
ANY = pl.BlockSpec(memory_space=pl.ANY)
PARAMS = pltpu.CompilerParams(vmem_limit_bytes=24 * 2**20)


def part_order():
    freq = np.arange(NF).reshape(2, 64, 1, 2)
    return np.concatenate([freq, freq + NF], axis=2).reshape(2 * NF)


def tables():
    angle = (np.arange(NT)[:, None] * np.arange(1, NF + 1)[None, :] % NT) * (2.0 * np.pi / NT)
    waves = np.concatenate([np.cos(angle), -np.sin(angle)], axis=1)[:, part_order()]
    forward = (waves / np.sqrt(NT)).astype(np.float32).astype(ml_dtypes.bfloat16)
    returned = np.concatenate([RETURNED, 256 + RETURNED])
    inverse = (waves[:, returned] * (2.0 / np.sqrt(NT))).astype(np.float32).astype(ml_dtypes.bfloat16)
    first = forward[: NT // 2]
    return np.ascontiguousarray(first.reshape(NT // 2, 2, 256).transpose(1, 0, 2)), np.ascontiguousarray(first.T), inverse


def one_hot(rows, depth):
    return np.eye(depth, dtype=np.float32)[np.asarray(rows).reshape(-1)].astype(ml_dtypes.bfloat16)


SHOT_MAJOR = one_hot(np.arange(256).reshape(64, 4).T, 256)
TIME_MAJOR = one_hot(np.arange(256).reshape(4, 64).T, 256)
def chip_order(turn, sign, axes=(0, 1, 2), stride=1):
    order = []
    for a in range(64):
        a = a * stride % 64
        at = [0, 0, 0]
        for axis, digit in zip(axes, (a // 16, a // 4 % 4, a % 4)):
            at[axis] = (turn[axis] + sign * digit) % 4
        z, y, x = at
        order.append(((4 * z + y) * 2 + x % 2, x // 2))
    return order


CHIPS_IN = chip_order((3, 2, 3), 1, (0, 1, 2), 21)
CHIPS_OUT = chip_order((2, 2, 2), 1, (2, 0, 1), 21)
RANK = np.zeros((32, 2), np.int64)
for rank, chip in enumerate(CHIPS_IN):
    RANK[chip] = rank
PART_MAJOR = one_hot(4 * RANK.T[None] + np.arange(4)[:, None, None], 256)
PART_SUM = (PART_MAJOR.reshape(4, 2, 32, 256)[:, 0] + PART_MAJOR.reshape(4, 2, 32, 256)[:, 1]).reshape(128, 256)
SPREAD = one_hot([[32 * o + shot for o in range(4)] for shot, _ in CHIPS_OUT], 128)
RETURNED = np.concatenate([4 * RANK[chip] + np.arange(4) for chip in CHIPS_OUT])


def exchange(x, chips):
    groups = [[(2 * shot + high) * 2 + core for shot, high in chips] for core in range(2)]
    return lax.all_to_all(x, ("shot", "xh", "core"), 0, 0, axis_index_groups=groups, tiled=True)


WIDE = NT // 4


def held(x):
    return pltpu.with_memory_space_constraint(x, pltpu.HBM)


def bin_sign():
    return (2 * (lax.broadcasted_iota(jnp.int32, (1, 256), 1) & 1) - 1).astype(F32).astype(BF16)


def record_spectra(rec, waves):
    total = None
    for k in range(4):
        wave = waves[WIDE * (k % 2) : WIDE * (k % 2) + WIDE]
        wave = wave if k < 2 else wave * bin_sign()
        part = jnp.dot(rec[:, :, WIDE * k : WIDE * k + WIDE].reshape(512, WIDE), wave, preferred_element_type=F32)
        total = part if total is None else total + part
    return total.T.astype(BF16)


def give_kernel(
    records_ref, table_ref, flipped_ref, aperture_ref, give_ref, picks_ref, rec, keep, piece_ref, tab, ape, sems
):
    core = lax.axis_index("core")
    small = pltpu.make_async_copy(aperture_ref, ape, sems.at[5])
    small.start()
    first = [pltpu.make_async_copy(table_ref.at[1 - core], tab, sems.at[0])]
    for c in range(2):
        first.append(pltpu.make_async_copy(records_ref.at[0, c], rec.at[c], sems.at[1 + c]))
    later = [
        pltpu.make_async_copy(table_ref.at[core], keep, sems.at[3]),
        pltpu.make_async_copy(flipped_ref.at[pl.ds(pl.multiple_of(core * 256, 256), 256)], piece_ref, sems.at[4]),
    ]
    for copy in first + later:
        copy.start()
    c = lax.broadcasted_iota(jnp.int32, (64, 64), 0)
    j = lax.broadcasted_iota(jnp.int32, (64, 64), 1)
    order = (c == 2 * (j & 31) + (j >> 5)).astype(F32).astype(BF16)
    small.wait()
    picks = jnp.dot(ape[...].reshape(4, 64).astype(F32).astype(BF16), order, preferred_element_type=F32).astype(BF16)
    picks_ref[...] = picks
    give_ref[256:272, :] = jnp.zeros((16, 512), BF16)
    give_ref[256:260, 0:64] = picks
    for copy in first:
        copy.wait()
    give_ref[0:256, :] = record_spectra(rec, tab)
    for copy in later:
        copy.wait()


def transform_given(records, table, flipped, aperture):
    return pl.pallas_call(
        give_kernel,
        out_shape=(
            jax.ShapeDtypeStruct((272, 512), BF16),
            jax.ShapeDtypeStruct((4, 64), BF16),
            jax.ShapeDtypeStruct((2, 256, NT), BF16),
            jax.ShapeDtypeStruct((NT // 2, 256), BF16),
            jax.ShapeDtypeStruct((256, 1024), BF16),
        ),
        in_specs=[ANY, ANY, ANY, ANY],
        out_specs=(VMEM, VMEM, VMEM, VMEM, VMEM),
        scratch_shapes=[
            pltpu.VMEM((NT // 2, 256), BF16),
            pltpu.VMEM((4, 1, 64), jnp.int32),
            pltpu.SemaphoreType.DMA((6,)),
        ],
        compiler_params=PARAMS,
        cost_estimate=pl.CostEstimate(flops=2**29, bytes_accessed=5 * 2**20, transcendentals=0),
        name="give",
    )(held(records), held(table), held(flipped), held(aperture))


def keep_kernel(rec_ref, keep_ref, own_ref, other_ref, piece_ref, order_ref, out_ref, flat):
    core = lax.axis_index("core")
    out_ref[:, :, 0:512] = record_spectra(rec_ref, keep_ref).reshape(64, 4, 512)
    total = None
    for i, raw_ref in enumerate((own_ref, other_ref)):
        for t in range(8):
            rows = jnp.dot(
                order_ref[...], raw_ref[64 * t : 64 * t + 64].reshape(256, 256), preferred_element_type=F32
            ).astype(BF16)
            for s in range(4):
                flat[i, 64 * t : 64 * t + 64, 256 * s : 256 * s + 256] = rows[64 * s : 64 * s + 64]
        at = core if i == 0 else 1 - core
        waves = piece_ref[:, pl.ds(pl.multiple_of(at * 512, 512), 512)]
        part = jnp.dot(waves, flat[i], preferred_element_type=F32)
        total = part if total is None else total + part
    odd = 1 - (lax.broadcasted_iota(jnp.int32, (256, 1), 0) & 1)
    total = total * (1 - 2 * odd * lax.axis_index("xh")).astype(F32)
    out_ref[:, :, 1024:2048] = total.astype(BF16).reshape(64, 4, 1024)


def transform_kept(rec, keep, own, other, piece):
    return pl.pallas_call(
        keep_kernel,
        out_shape=jax.ShapeDtypeStruct((64, 4, 2176), BF16),
        in_specs=[VMEM] * 6,
        out_specs=VMEM,
        scratch_shapes=[pltpu.VMEM((2, 512, 1024), BF16)],
        compiler_params=PARAMS,
        cost_estimate=pl.CostEstimate(flops=3 * 2**29, bytes_accessed=4 * 2**20, transcendentals=0),
        name="keep",
    )(rec, keep, own, other, piece, SHOT_MAJOR)


def fill_kernel(message_ref, taken_ref, picks_ref, out_ref, block, picks, sems):
    block[...] = taken_ref[0:256, :].reshape(64, 4, 512)
    both = jnp.concatenate([picks_ref[...], taken_ref[256:260, 0:64]], axis=1)
    picks[...] = jnp.broadcast_to(both[None], (64, 4, 128))
    first = pltpu.make_async_copy(block, out_ref.at[:, :, 512:1024], sems.at[0])
    second = pltpu.make_async_copy(picks, out_ref.at[:, :, 2048:2176], sems.at[1])
    first.start()
    second.start()
    first.wait()
    second.wait()


def fill(message, taken, picks):
    return pl.pallas_call(
        fill_kernel,
        out_shape=jax.ShapeDtypeStruct((64, 4, 2176), BF16),
        in_specs=[ANY, VMEM, VMEM],
        out_specs=ANY,
        scratch_shapes=[
            pltpu.VMEM((64, 4, 512), BF16),
            pltpu.VMEM((64, 4, 128), BF16),
            pltpu.SemaphoreType.DMA((2,)),
        ],
        input_output_aliases={0: 0},
        compiler_params=PARAMS,
        name="fill",
    )(message, taken, picks)


def lane_pick(low, high, index):
    inside = index & 127
    a = jnp.take_along_axis(low, inside, axis=1, mode="promise_in_bounds")
    b = jnp.take_along_axis(high, inside, axis=1, mode="promise_in_bounds")
    return jnp.where(index < 128, a, b)


def mix_kernel(got_ref, order_ref, both_ref, spread_ref, out_ref):
    order = order_ref[...]
    rows = jnp.dot(order, got_ref[:, :, 0:1024].reshape(256, 1024), preferred_element_type=F32).astype(BF16)
    shots = jnp.dot(both_ref[...], got_ref[:, :, 1024:2048].reshape(256, 1024), preferred_element_type=F32)
    where = jnp.dot(order, got_ref[:, :, 2048:2176].reshape(256, 128), preferred_element_type=F32).astype(jnp.int32)
    picks, gathers = [], []
    for p in range(4):
        parts = []
        for s in range(4):
            low = shots[32 * p : 32 * p + 32, 256 * s : 256 * s + 128]
            high = shots[32 * p : 32 * p + 32, 256 * s + 128 : 256 * s + 256]
            parts.append(
                jnp.concatenate(
                    [lane_pick(low, high, where[64 * s + 32 * h : 64 * s + 32 * h + 32]) for h in range(2)], axis=1
                )
            )
        picks.append(jnp.concatenate(parts, axis=0))
        gathers.append(
            jnp.concatenate(
                [
                    rows[64 * p + 32 * h : 64 * p + 32 * h + 32, 256 * b : 256 * b + 256]
                    for h in range(2)
                    for b in range(4)
                ],
                axis=0,
            )
        )
    total = [None] * 4
    for f in range(2):
        re, im, minus = picks[f].astype(BF16), picks[2 + f].astype(BF16), (-picks[2 + f]).astype(BF16)
        left = jnp.concatenate(
            [jnp.concatenate([re, minus], axis=1), jnp.concatenate([im, re], axis=1)], axis=0
        )
        right = jnp.concatenate([gathers[f], gathers[2 + f]], axis=0)
        out = jnp.dot(left, right, preferred_element_type=F32).astype(BF16)
        for part in range(2):
            total[2 * part + f] = jnp.concatenate(
                [out[128 * part + 32 * s : 128 * part + 32 * s + 32] for s in range(4)], axis=1
            )
    total = jnp.concatenate(total, axis=0)
    out_ref[...] = (
        jnp.dot(spread_ref[...], total, preferred_element_type=F32).astype(BF16).reshape(64, 4, 1024)
    )


def mix(got):
    return pl.pallas_call(
        mix_kernel,
        out_shape=jax.ShapeDtypeStruct((64, 4, 1024), BF16),
        in_specs=[VMEM, VMEM, VMEM, VMEM],
        out_specs=VMEM,
        compiler_params=PARAMS,
        name="mix",
    )(got, PART_MAJOR, PART_SUM, SPREAD)


def inverse_waves(table_ref, half, rows, count):
    block = 2 * lax.axis_index("xh") + lax.axis_index("core")
    return table_ref[
        pl.ds(pl.multiple_of(block * 512 + rows, 256), count), pl.ds(pl.multiple_of(half * 256, 256), 256)
    ]


def own_half_kernel(own_ref, table_ref, out_ref):
    waves = inverse_waves(table_ref, lax.axis_index("core"), 0, 512)
    out_ref[...] = jnp.dot(waves, own_ref[...].reshape(256, 1024), preferred_element_type=F32)


def own_half(own, table):
    return pl.pallas_call(
        own_half_kernel,
        out_shape=jax.ShapeDtypeStruct((512, 1024), F32),
        in_specs=[VMEM, VMEM],
        out_specs=VMEM,
        compiler_params=PARAMS,
        cost_estimate=pl.CostEstimate(flops=2**28, bytes_accessed=2**20, transcendentals=0),
        name="own_half",
    )(own, table)


def inverse_kernel(part_ref, other_ref, table_ref, order_ref, out_ref, ready, sems):
    other = other_ref[...].reshape(256, 1024)
    outs = []
    for half in range(2):
        waves = inverse_waves(table_ref, 1 - lax.axis_index("core"), 256 * half, 256)
        here = jnp.dot(waves, other, preferred_element_type=F32)
        here = (here + part_ref[256 * half : 256 * half + 256]).astype(BF16)
        for t in range(4):
            at = 256 * half + 64 * t
            stack = jnp.concatenate(
                [here[64 * t : 64 * t + 64, 256 * s : 256 * s + 256] for s in range(4)], axis=0
            )
            ready[at : at + 64] = (
                jnp.dot(order_ref[...], stack, preferred_element_type=F32).astype(BF16).reshape(64, 4, 256)
            )
            if t >= 0:
                rows = pl.ds(at, 64)
                outs.append(pltpu.make_async_copy(ready.at[rows], out_ref.at[rows], sems.at[len(outs)]))
                outs[-1].start()
    for copy in outs:
        copy.wait()


def transform_back(part, other, table):
    return pl.pallas_call(
        inverse_kernel,
        out_shape=jax.ShapeDtypeStruct((512, 4, 256), BF16),
        in_specs=[VMEM, VMEM, VMEM, VMEM],
        out_specs=ANY,
        scratch_shapes=[pltpu.VMEM((512, 4, 256), BF16), pltpu.SemaphoreType.DMA((8,))],
        compiler_params=PARAMS,
        name="inverse",
    )(part, other, table, TIME_MAJOR)


def on_device(records, targets, aperture):
    forward, flipped, inverse = tables()
    swap = [(0, 1), (1, 0)]
    others = lax.ppermute(targets, "core", swap)
    give, picks, rec, keep, piece = transform_given(records, forward, flipped, aperture)
    taken = lax.ppermute(give, "core", swap)
    message = transform_kept(rec, keep, targets, others, piece)
    message = fill(message, taken, picks)
    back = exchange(mix(exchange(message, CHIPS_IN)), CHIPS_OUT)
    other = lax.ppermute(back, "core", swap)
    return transform_back(own_half(back, inverse), other, inverse)


def solution(mesh):
    cut = Mesh(mesh.devices.reshape(32, 2, 2), ("shot", "xh", "core"))
    xline = ("xh", "core")
    return jax.shard_map(
        on_device,
        mesh=cut,
        in_specs=(P(xline, "shot", None, None), P(xline, "shot", None), P("shot", xline, None)),
        out_specs=P(xline, "shot", None),
        check_vma=False,
    )
```
